256 devices in a mesh: tensor: 32 (over y, x, z_lo), section: 8 (over z_hi, core).
Axes of the slice: x: 4, y: 4, z: 8 (z_hi: 4, z_lo: 2; z = z_hi * 2 + z_lo), core: 2. Of those that a mesh axis runs over, the one named last changes fastest.
Arguments:
- resid: bfloat16 [8, 384, 8192], P('section', 'tensor'), may hold values from -6 to 6
- norm_gain: float32 [8192], replicated, may hold values from 0.1 to 1.9
- signs: int32 [8192], replicated, may hold values from 0 to 1
- query_weight: bfloat16 [8192, 8192], P(None, 'tensor'), may hold values from -0.30935922 to 0.30935922
- kv_weight: bfloat16 [8192, 2048], P(None, 'tensor'), may hold values from -0.30935922 to 0.30935922
- out_weight: bfloat16 [8192, 8192], P('tensor'), may hold values from -0.25 to 0.25
- lengths: int32 [8], replicated, may hold values from 1 to 384, 2304 in all
Outputs:
- mixed: bfloat16 [8, 384, 8192], P('section', 'tensor')
The draws below stay inside these ranges and needn't reach their ends.
Inputs may be any that keep to these rules, and one draw needn't show every extreme that they name: Block c holds lengths[c] valid tokens at its start and padding after them; the lengths sum to 2304 and at least one block is full.
All inputs are finite; a program needn't handle non-finite values.
Results may differ from the reference program's by a relative error of at most 0.025.
Values may be sent and summed in bfloat16 or wider, within the bound.
A program may use at most 128 MiB of HBM per device.

```python
import math
import jax
import jax.numpy as jnp
import numpy as np
from jax import lax

D = 8192
H = 64
KVH = 8
HD = 128
HB = 128
TOK = 384
BLOCKS = 8
SEQ = 3072
VALID = 2304
N_TENSOR = 32


def draw_query_weight(key, part):
    key = jax.random.fold_in(key, 1)
    matrix = jnp.clip(jax.random.normal(key, (D, KVH, H // KVH, HD), jnp.float32), -4.0, 4.0)
    return (matrix.reshape(D, H * HD) / math.sqrt(D)).astype(jnp.bfloat16)


def draw_kv_weight(key, part):
    key = jax.random.fold_in(key, 2)
    matrix = jnp.clip(jax.random.normal(key, (D, KVH, 2, HD), jnp.float32), -4.0, 4.0)
    return (matrix.reshape(D, 2 * KVH * HD) / math.sqrt(D)).astype(jnp.bfloat16)


def set_ends(values, stream_key, least, high):
    shape = values.shape
    spot = [jax.random.randint(jax.random.fold_in(stream_key, axis), (), 0, shape[axis]) for axis in range(len(shape))]
    values = values.at[tuple(spot)].set(least)
    longest = shape.index(max(shape))
    spot[longest] = (spot[longest] + 1) % shape[longest]
    return values.at[tuple(spot)].set(high)


def levels(own_key, dims, split, low, top_value):
    gain, own = 1.0, jax.random.fold_in(own_key, 6)
    for position, shards_of in split:
        heights = jnp.exp(jax.random.uniform(jax.random.fold_in(own, position), (shards_of,), jnp.float32, low / len(split), top_value / len(split)))
        gain = gain * jnp.repeat(heights, dims[position] // shards_of).reshape([-1 if axis == position else 1 for axis in range(len(dims))])
    return gain


def profile(amount, total, reach, skew):
    portions = [(1 << 20) // math.isqrt(rank ** skew) + 1 for rank in range(2, amount + 1)]
    surplus, given = total - reach - (amount - 1), [1] * (amount - 1)
    while surplus > 0:
        free = [i for i in range(amount - 1) if given[i] < reach]
        whole, left = sum([portions[i] for i in free]), surplus
        for i in free:
            addition = min(reach - given[i], max(1, left * portions[i] // whole), surplus)
            given[i] = given[i] + addition
            surplus = surplus - addition
    return np.array([reach] + given)


def ragged(rng, amount, total, reach, slope):
    if amount == 2:
        one = jax.random.randint(rng, (), max(1, total - reach), min(reach, total - 1) + 1)
        return jnp.stack([one, total - one])
    sizes = jnp.asarray(profile(amount, total, reach, slope), jnp.int32)
    couples = (amount - 1) // 2
    source_of, taker = sizes[1:1 + 2 * couples:2], sizes[2:2 + 2 * couples:2]
    slack = jnp.minimum(source_of - 1, reach - taker)
    passed = jax.random.randint(jax.random.fold_in(rng, 1), (couples,), 0, 1 << 20) % (slack + 1)
    sizes = sizes.at[1:1 + 2 * couples:2].set(source_of - passed).at[2:2 + 2 * couples:2].set(taker + passed)
    return sizes[jax.random.permutation(jax.random.fold_in(rng, 2), amount)]


def noise(rng, dims, width, bound, split=(), held_as=jnp.bfloat16):
    gain = levels(rng, dims, split, -0.22, 0.18) if split else 1.0
    drawn = jax.random.normal(rng, dims, jnp.float32) * width * gain
    return jnp.minimum(jnp.maximum(drawn, -bound), bound).astype(held_as)


def setup_inputs(seed: int = 0) -> dict:
    arg_keys = jax.random.split(jax.random.key(seed), 8)
    return {
        "resid": noise(arg_keys[0], (BLOCKS, TOK, D), 1.0, 6.0, ((0, 8), (1, 32))),
        "norm_gain": jnp.clip(1.0 + 0.18 * jax.random.normal(arg_keys[1], (D,), jnp.float32), 0.1, 1.9),
        "signs": set_ends(jax.random.randint(arg_keys[2], (D,), 0, 2), jax.random.fold_in(arg_keys[2], 1), 0, 1).astype(jnp.int32),
        "query_weight": draw_query_weight(jax.random.fold_in(arg_keys[7], 71), 0),
        "kv_weight": draw_kv_weight(jax.random.fold_in(arg_keys[7], 71), 0),
        "out_weight": noise(arg_keys[5], (H * HD, D), (H * HD // 16) ** -0.5, 0.25, ((0, 32),)),
        "lengths": ragged(arg_keys[6], BLOCKS, VALID, TOK, 1).astype(jnp.int32),
    }


rope_base = 500000.0
norm_eps = 1e-05

def hadamard_table(extent):
    index = jnp.arange(extent, dtype=jnp.int32)
    parity = jnp.zeros((extent, extent), jnp.int32)
    bit_value = 1
    while bit_value < extent:
        row_bit = index // bit_value % 2
        parity = parity + row_bit[:, None] * row_bit[None, :]
        bit_value = bit_value * 2
    return (1 - 2 * (parity % 2)).astype(jnp.float32)

def rotate_blocks(values, sign_row, hadamard):
    row_count = values.shape[0]
    grouped = (values * sign_row).reshape(row_count, -1, hadamard.shape[0])
    result = jnp.einsum('rbj,ji->rbi', grouped, hadamard, precision=lax.Precision.HIGHEST)
    return result.reshape(row_count, -1) / math.sqrt(hadamard.shape[0])

def unrotate_blocks(values, sign_row, hadamard):
    row_count = values.shape[0]
    grouped = values.reshape(row_count, -1, hadamard.shape[0])
    result = jnp.einsum('rbi,ji->rbj', grouped, hadamard, precision=lax.Precision.HIGHEST)
    return result.reshape(row_count, -1) / math.sqrt(hadamard.shape[0]) * sign_row

def rotary(inputs, float_pos):
    half_dim = inputs.shape[-1] // 2
    inverse_freq = jnp.exp(jnp.arange(half_dim, dtype=jnp.float32) * (-2.0 * math.log(rope_base) / inputs.shape[-1]))
    angles = float_pos[:, None] * inverse_freq[None, :]
    cosine = jnp.cos(angles)[:, None, :]
    sine_part = jnp.sin(angles)[:, None, :]
    first_half = inputs[..., :half_dim]
    second_half = inputs[..., half_dim:]
    return jnp.concatenate([first_half * cosine - second_half * sine_part, second_half * cosine + first_half * sine_part], axis=-1)

def reference(resid, norm_gain, signs, query_weight, kv_weight, out_weight, lengths):
    hadamard = jnp.asarray(hadamard_table(HB), jnp.float32)
    sign_row = (2 * signs - 1).astype(jnp.float32)
    stream = resid.reshape(SEQ, D).astype(jnp.float32)
    normed = stream * lax.rsqrt(lax.optimization_barrier(jnp.mean(stream * stream, axis=-1, keepdims=True)) + norm_eps) * norm_gain
    rotated = rotate_blocks(normed, sign_row, hadamard).astype(jnp.bfloat16)
    offsets = (jnp.cumsum(lengths) - lengths).astype(jnp.int32)
    block_of = (jnp.arange(SEQ) // TOK).astype(jnp.int32)
    token_of = (jnp.arange(SEQ) % TOK).astype(jnp.int32)
    positions = offsets[block_of] + token_of
    float_pos = positions.astype(jnp.float32)
    queries = rotary(jnp.dot(rotated, query_weight, preferred_element_type=jnp.float32).reshape(SEQ, H, HD), float_pos).astype(jnp.bfloat16)
    kv_proj = jnp.dot(rotated, kv_weight, preferred_element_type=jnp.float32).astype(jnp.bfloat16).reshape(SEQ, KVH, 2, HD)
    key_rows = rotary(kv_proj[:, :, 0].astype(jnp.float32), float_pos).astype(jnp.bfloat16)
    value_rows = kv_proj[:, :, 1]
    key_valid = token_of < lengths[block_of]
    earlier = block_of[None, :] < block_of[:, None]
    same_block = (block_of[None, :] == block_of[:, None]) & (token_of[None, :] <= token_of[:, None])
    visible = key_valid[None, :] & (earlier | same_block)
    group_size = H // KVH
    query_groups = queries.reshape(SEQ, KVH, group_size, HD).transpose(1, 2, 0, 3)

    def attend_group(operands):
        query_block, key_block, value_block = operands
        scores = jnp.einsum('gqd,kd->gqk', query_block.astype(jnp.float32), key_block.astype(jnp.float32)) / math.sqrt(HD)
        row_max = lax.optimization_barrier(jnp.max(jnp.where(visible[None], scores, -jnp.inf), axis=-1, keepdims=True))
        weights = jnp.where(visible[None], jnp.exp(scores - row_max), 0.0)
        rounded = weights.astype(jnp.bfloat16)
        summed = jnp.einsum('gqk,kd->gqd', rounded.astype(jnp.float32), value_block.astype(jnp.float32))
        return (summed / lax.optimization_barrier(jnp.sum(weights, axis=-1, keepdims=True))).astype(jnp.bfloat16)
    attended = lax.map(attend_group, (query_groups, key_rows.transpose(1, 0, 2), value_rows.transpose(1, 0, 2)))
    attended = attended.transpose(2, 0, 1, 3).reshape(SEQ, H * HD)
    part_width = H * HD // N_TENSOR
    attended_parts = attended.reshape(SEQ, N_TENSOR, part_width).transpose(1, 0, 2)
    weight_parts = out_weight.reshape(N_TENSOR, part_width, D)

    def add_part(running, operands):
        attended_part, weight_part = operands
        partial_value = jnp.dot(attended_part, weight_part, preferred_element_type=jnp.float32).astype(jnp.bfloat16)
        return (running + lax.optimization_barrier(partial_value).astype(jnp.float32), None)
    branch, _ = lax.scan(add_part, jnp.zeros((SEQ, D), jnp.float32), (attended_parts, weight_parts))
    mixed = stream + unrotate_blocks(branch, sign_row, hadamard)
    return mixed.astype(jnp.bfloat16).reshape(BLOCKS, TOK, D)
```

```python
import functools
import math

import jax
import jax.numpy as jnp
import numpy as np
from jax import lax
from jax.experimental import pallas as pl
from jax.experimental.pallas import tpu as pltpu
from jax.sharding import PartitionSpec as P

MESH = pl.DeviceIdType.MESH
D = 8192
HD = 128
HB = 128
ROWS = 12
TOK = 384
BLOCKS = 8
NC = 4
CW = D // NC
SUB = 4
SW = CW // SUB
PR = SUB * ROWS
QC = 256
KC = 64
rope_base = 500000.0
norm_eps = 1e-05
NEG = -1e30


def hadamard(extent):
    index = np.arange(extent)
    bits = index[:, None] & index[None, :]
    parity = np.zeros((extent, extent), np.int64)
    while bits.any():
        parity += bits & 1
        bits = bits >> 1
    return (1 - 2 * (parity % 2)).astype(np.float32)


def token_order():
    order = []
    for half in range(2):
        for j in range(4):
            for i in range(4):
                y, x = (j, i) if half == 0 else (i, j)
                t = (y * 4 + x) * 2 + half
                order.extend(range(t * ROWS, (t + 1) * ROWS))
    return np.array(order)


def here():
    t = lax.axis_index("tensor")
    s = lax.axis_index("section")
    y = t // 8
    x = lax.rem(t // 2, 4)
    z = (s // 2) * 2 + lax.rem(t, 2)
    return y, x, z, lax.rem(s, 2)


def device(y, x, z, c):
    return ((y * 4 + x) * 2 + lax.rem(z, 2), (z // 2) * 2 + c)


def shift(value, by, size):
    return lax.rem(value + (by + size), size)


def split3(value):
    high = value.astype(jnp.bfloat16)
    rest = value - high.astype(jnp.float32)
    middle = rest.astype(jnp.bfloat16)
    low = (rest - middle.astype(jnp.float32)).astype(jnp.bfloat16)
    return jnp.concatenate([high, middle, low], axis=1)


def greet(partners):
    barrier = pltpu.get_barrier_semaphore()
    for partner in partners:
        pl.semaphore_signal(barrier, inc=1, device_id=partner, device_id_type=MESH)
    pl.semaphore_wait(barrier, len(partners))


def remote(src, dst, send, recv, target):
    return pltpu.make_async_remote_copy(
        src_ref=src,
        dst_ref=dst,
        send_sem=send,
        recv_sem=recv,
        device_id=target,
        device_id_type=MESH,
    )


def project_kernel(
    resid, gain_sign, had, q_hbm, kv_hbm, cos_ref, sin_ref, q_out, kv_out,
    wq, wkv, p2, blocks, acc_q, acc_kv, w_sem, sz, rz, s2, r2, s3, r3,
):
    y, x, z, core = here()
    low = lax.rem(z, 2)
    mate = z + 1 - 2 * low

    def inner(h, by):
        return device(shift(y, by * h, 4), shift(x, by * (1 - h), 4), z, core)

    def outer(h, by):
        return device(shift(y, by * (1 - h), 4), shift(x, by * h, 4), z, core)

    def inner_pos(h):
        return x * (1 - h) + y * h

    def outer_pos(h):
        return y * (1 - h) + x * h

    greet(
        [device(y, x, mate, core)]
        + [inner(h, by) for h in range(2) for by in (1, -1)]
    )
    loads = [
        pltpu.make_async_copy(q_hbm, wq, w_sem.at[0]),
        pltpu.make_async_copy(kv_hbm, wkv, w_sem.at[1]),
    ]
    for load in loads:
        load.start()

    stream = resid[0].astype(jnp.float32)
    normed = (
        stream
        * lax.rsqrt(jnp.mean(stream * stream, axis=-1, keepdims=True) + norm_eps)
        * gain_sign[...]
    )
    stacked = []
    for c in range(NC):
        for b in range(SW // HB):
            stacked.append(
                jnp.concatenate(
                    [
                        normed[:, c * CW + j * SW + b * HB : c * CW + j * SW + (b + 1) * HB]
                        for j in range(SUB)
                    ],
                    axis=0,
                )
            )
    stacked = jnp.concatenate(stacked, axis=0)
    rotated = jnp.dot(split3(stacked), had[...], preferred_element_type=jnp.float32) * (
        1.0 / math.sqrt(HB)
    )
    own_pos = inner_pos(low)
    for c in range(NC):
        parts = [
            rotated[(c * (SW // HB) + b) * PR : (c * (SW // HB) + b + 1) * PR]
            for b in range(SW // HB)
        ]
        p2[low, own_pos, c] = jnp.concatenate(parts, axis=1).astype(jnp.bfloat16)

    started = []

    def go(copy):
        copy.start()
        started.append(copy)

    def z_copy(c, half):
        ref = p2.at[half, inner_pos(half), c]
        return remote(ref, ref, sz.at[c], rz.at[c], device(y, x, mate, core))

    def direct2(h, c):
        ref = p2.at[h, inner_pos(h), c]
        go(remote(ref, ref, s2.at[h, 0, c], r2.at[h, 0, c], inner(h, 1)))
        go(remote(ref, ref, s2.at[h, 1, c], r2.at[h, 1, c], inner(h, -1)))

    def direct3(h, c):
        ref = blocks.at[h, outer_pos(h), c]
        go(remote(ref, ref, s3.at[h, 0, c], r3.at[h, 0, c], outer(h, 1)))
        go(remote(ref, ref, s3.at[h, 1, c], r3.at[h, 1, c], outer(h, -1)))

    def arrive(buf, pos, ssem, rsem, peer, h, c):
        for kind, by in ((0, -1), (1, 1)):
            ref = buf.at[h, shift(pos(h), by, 4), c]
            remote(ref, ref, ssem.at[h, kind, c], rsem.at[h, kind, c], peer(h, 1)).wait_recv()
        by = -1 if c % 2 == 0 else 1
        ref = buf.at[h, shift(pos(h), by, 4), c]
        go(remote(ref, ref, ssem.at[h, 2, c], rsem.at[h, 2, c], peer(h, -by)))

    def last(buf, pos, ssem, rsem, peer, h, c):
        ref = buf.at[h, shift(pos(h), 2, 4), c]
        remote(ref, ref, ssem.at[h, 2, c], rsem.at[h, 2, c], peer(h, 1)).wait_recv()

    for c in range(NC):
        go(z_copy(c, low))
        direct2(low, c)
    for c in range(NC):
        z_copy(c, 1 - low).wait_recv()
        direct2(1 - low, c)
    for c in range(NC + 1):
        if c < NC:
            for h in range(2):
                arrive(p2, inner_pos, s2, r2, inner, h, c)
        if c > 0:
            for h in range(2):
                last(p2, inner_pos, s2, r2, inner, h, c - 1)
                pieces = [p2[h, i, c - 1].astype(jnp.float32) for i in range(4)]
                joined = jnp.concatenate(
                    [
                        jnp.concatenate(
                            [piece[j * ROWS : (j + 1) * ROWS] for piece in pieces], axis=0
                        )
                        for j in range(SUB)
                    ],
                    axis=1,
                )
                blocks[h, outer_pos(h), c - 1] = joined.astype(jnp.bfloat16)
                direct3(h, c - 1)
    for load in loads:
        load.wait()
    for c in range(NC + 1):
        if c < NC:
            for h in range(2):
                arrive(blocks, outer_pos, s3, r3, outer, h, c)
        if c > 0:
            for h in range(2):
                last(blocks, outer_pos, s3, r3, outer, h, c - 1)
            left = blocks[:, :, c - 1].reshape(TOK, CW)
            rows = pl.ds((c - 1) * CW, CW)
            part_q = jnp.dot(left, wq[rows], preferred_element_type=jnp.float32)
            part_kv = jnp.dot(left, wkv[rows], preferred_element_type=jnp.float32)
            if c == 1:
                acc_q[...] = part_q
                acc_kv[...] = part_kv
            else:
                acc_q[...] += part_q
                acc_kv[...] += part_kv
    kv_out[...] = jnp.transpose(acc_kv[...]).astype(jnp.bfloat16)
    turned = jnp.transpose(acc_q[...])
    cosine, sine = cos_ref[...], sin_ref[...]
    half = HD // 2
    for head in range(2):
        first = turned[head * HD : head * HD + half]
        second = turned[head * HD + half : (head + 1) * HD]
        q_out[head * HD : head * HD + half] = (first * cosine - second * sine).astype(jnp.bfloat16)
        q_out[head * HD + half : (head + 1) * HD] = (second * cosine + first * sine).astype(
            jnp.bfloat16
        )
    for copy in started:
        copy.wait_send()


def attend_kernel(
    lengths, q_ref, kv_ref, off_cos, off_sin, tok_cos, tok_sin, key_tok, query_tok,
    out_hbm, resid, sign_row, had, mixed,
    wo, kvs, att, parts, raw1, fin1, parts2, raw2, fin2, sums, sums_bf, last_z, acc,
    w_sem, sx, rx, skv, rkv, sc, rc, s1, r1, s2, r2, sz, rz,
):
    y, x, z, core = here()
    low = lax.rem(z, 2)
    mate = z + 1 - 2 * low
    section = lax.axis_index("section")

    def inner(h, by):
        return device(shift(y, by * (1 - h), 4), shift(x, by * h, 4), z, core)

    def outer(h, by):
        return device(shift(y, by * h, 4), shift(x, by * (1 - h), 4), z, core)

    def inner_pos(h):
        return y * (1 - h) + x * h

    def outer_pos(h):
        return x * (1 - h) + y * h

    def along(by):
        return device(y, x, shift(z, by, 8), core)

    other_core = device(y, x, z, 1 - core)
    own_x = lax.rem(x, 2)
    x_mate = device(y, x + 1 - 2 * own_x, z, core)
    greet([along(1), along(-1), other_core] + [inner(h, by) for h in range(2) for by in (1, -1)])
    load = pltpu.make_async_copy(out_hbm, wo, w_sem)
    load.start()
    started = []

    def go(copy):
        copy.start()
        started.append(copy)

    def side(e):
        return own_x if e == 0 else 1 - own_x

    def hop(e, src_by, kind, dist, target):
        ref = kvs.at[core, side(e), shift(z, src_by, 8)]
        return remote(ref, ref, skv.at[kind, dist, e], rkv.at[kind, dist, e], target)

    def to_core(e, src_by):
        k = src_by % 8
        ref = kvs.at[core, side(e), shift(z, src_by, 8)]
        go(remote(ref, ref, sc.at[e, k], rc.at[e, k], other_core))

    kvs[core, own_x, z] = kv_ref[...]
    own = kvs.at[core, own_x, z]
    go(remote(own, own, sx, rx, x_mate))
    go(hop(0, 0, 0, 0, along(1)))
    go(hop(0, 0, 1, 0, along(-1)))
    to_core(0, 0)
    theirs = kvs.at[core, 1 - own_x, z]
    remote(theirs, theirs, sx, rx, x_mate).wait_recv()
    go(hop(1, 0, 0, 0, along(1)))
    go(hop(1, 0, 1, 0, along(-1)))
    to_core(1, 0)
    for dist in range(4):
        for e in range(2):
            for kind, sgn in ((0, -1), (1, 1)):
                if dist == 3 and kind != e:
                    continue
                by = sgn * (dist + 1)
                hop(e, by, kind, dist, along(1)).wait_recv()
                if dist < 2 or (dist == 2 and kind == e):
                    go(hop(e, by, kind, dist + 1, along(-sgn)))
                to_core(e, by)
    for e in range(2):
        for k in range(8):
            ref = kvs.at[1 - core, side(e), shift(z, k, 8)]
            remote(ref, ref, sc.at[e, k], rc.at[e, k], other_core).wait_recv()

    scale = math.log2(math.e) / math.sqrt(HD)
    half = HD // 2

    def block(index):
        c = lax.rem(index, 2)
        pair = pl.ds((index // 2) * 2, 2)
        raw = kvs[c, 0, pair].astype(jnp.float32)
        value = kvs[c, 1, pair].reshape(HD, TOK)
        oc, os = off_cos[index], off_sin[index]
        cosine = oc * tok_cos[...] - os * tok_sin[...]
        sine = os * tok_cos[...] + oc * tok_sin[...]
        first, second = raw[0], raw[1]
        key = jnp.concatenate(
            [first * cosine - second * sine, second * cosine + first * sine], axis=0
        )
        key = jnp.transpose(key).astype(jnp.bfloat16)
        query = q_ref[...]
        scores = jnp.concatenate(
            [
                jnp.dot(key, query[:HD], preferred_element_type=jnp.float32),
                jnp.dot(key, query[HD:], preferred_element_type=jnp.float32),
            ],
            axis=1,
        )
        return scores, value

    scores, value = block(section)
    seen = (key_tok[...] < lengths[section]) & (key_tok[...] <= query_tok[...])
    scores = jnp.where(seen, scores, NEG)
    top = jnp.max(scores, axis=0, keepdims=True)
    weights = jnp.where(seen, jnp.exp2((scores - top) * scale), 0.0)
    total = jnp.sum(weights, axis=0, keepdims=True)
    acc[...] = jnp.dot(value, weights.astype(jnp.bfloat16), preferred_element_type=jnp.float32)

    def step(index, carry):
        top, total = carry
        scores, value = block(index)
        scores = scores + jnp.where(key_tok[...] < lengths[index], 0.0, NEG)
        new_top = jnp.maximum(top, jnp.max(scores, axis=0, keepdims=True))
        weights = jnp.exp2((scores - new_top) * scale)
        fade = jnp.exp2((top - new_top) * scale)
        acc[...] = acc[...] * fade + jnp.dot(
            value, weights.astype(jnp.bfloat16), preferred_element_type=jnp.float32
        )
        return new_top, total * fade + jnp.sum(weights, axis=0, keepdims=True)

    top, total = lax.fori_loop(0, section, step, (top, total))
    attended = acc[...] / total
    for head in range(2):
        att[:, head * HD : (head + 1) * HD] = jnp.transpose(
            attended[:, head * TOK : (head + 1) * TOK]
        ).astype(jnp.bfloat16)

    def send_raw(buf, raw, pos, ssem, rsem, peer, h, c):
        by = 1 if c % 2 == 0 else -1
        go(
            remote(
                buf.at[h, shift(pos(h), 2, 4), c], raw.at[h, c], ssem.at[h, 2, c],
                rsem.at[h, 2, c], peer(h, by),
            )
        )

    def send_fin(buf, fin, pos, ssem, rsem, peer, h, c, kind):
        by = 1 if kind == 0 else -1
        go(
            remote(
                buf.at[h, shift(pos(h), by, 4), c], fin.at[h, kind, c], ssem.at[h, kind, c],
                rsem.at[h, kind, c], peer(h, by),
            )
        )

    def pass_on(buf, raw, fin, pos, ssem, rsem, peer, h, c):
        kind, by = (0, 1) if c % 2 == 0 else (1, -1)
        ref = raw.at[h, c]
        remote(ref, ref, ssem.at[h, 2, c], rsem.at[h, 2, c], peer(h, 1)).wait_recv()
        slot = shift(pos(h), by, 4)
        buf[h, slot, c] = (
            buf[h, slot, c].astype(jnp.float32) + raw[h, c].astype(jnp.float32)
        ).astype(jnp.bfloat16)
        send_fin(buf, fin, pos, ssem, rsem, peer, h, c, kind)

    def finish(buf, fin, pos, ssem, rsem, peer, h, c):
        for kind in range(2):
            ref = fin.at[h, kind, c]
            remote(ref, ref, ssem.at[h, kind, c], rsem.at[h, kind, c], peer(h, 1)).wait_recv()
        return (
            buf[h, pos(h), c].astype(jnp.float32)
            + fin[h, 0, c].astype(jnp.float32)
            + fin[h, 1, c].astype(jnp.float32)
        )

    ring1 = (inner_pos, s1, r1, inner)
    ring2 = (outer_pos, s2, r2, outer)
    load.wait()
    for c in range(NC):
        partial = jnp.dot(
            att[...], wo[:, c * CW : (c + 1) * CW], preferred_element_type=jnp.float32
        ).astype(jnp.bfloat16)
        parts[:, :, c] = partial.reshape(2, 4, PR, CW)
        for h in range(2):
            send_raw(parts, raw1, *ring1, h, c)
            send_fin(parts, fin1, *ring1, h, c, 1 if c % 2 == 0 else 0)
    for c in range(NC):
        for h in range(2):
            pass_on(parts, raw1, fin1, *ring1, h, c)

    def z_copy(c, half):
        return remote(
            sums_bf.at[half, c], last_z.at[c], sz.at[c], rz.at[c], device(y, x, mate, core)
        )

    for c in range(NC + 2):
        if c < NC:
            for h in range(2):
                done = finish(parts, fin1, *ring1, h, c)
                for i in range(4):
                    parts2[h, i, c] = jnp.concatenate(
                        [
                            done[i * ROWS : (i + 1) * ROWS, j * SW : (j + 1) * SW]
                            for j in range(SUB)
                        ],
                        axis=0,
                    ).astype(jnp.bfloat16)
                send_raw(parts2, raw2, *ring2, h, c)
                send_fin(parts2, fin2, *ring2, h, c, 1 if c % 2 == 0 else 0)
        if 0 < c <= NC:
            for h in range(2):
                pass_on(parts2, raw2, fin2, *ring2, h, c - 1)
        if c > 1:
            for h in range(2):
                done = finish(parts2, fin2, *ring2, h, c - 2)
                sums[h, c - 2] = done
                sums_bf[h, c - 2] = done.astype(jnp.bfloat16)
            go(z_copy(c - 2, 1 - low))
    stacked = []
    for c in range(NC):
        z_copy(c, low).wait_recv()
        branch = sums[low, c] + last_z[c].astype(jnp.float32)
        stacked += [branch[:, b * HB : (b + 1) * HB] for b in range(SW // HB)]
    stacked = jnp.concatenate(stacked, axis=0)
    back = jnp.dot(split3(stacked), had[...], preferred_element_type=jnp.float32) * (
        1.0 / math.sqrt(HB)
    )
    columns = []
    for c in range(NC):
        for j in range(SUB):
            for b in range(SW // HB):
                row = (c * (SW // HB) + b) * PR + j * ROWS
                columns.append(back[row : row + ROWS])
    back = jnp.concatenate(columns, axis=1)
    mixed[0] = (resid[0].astype(jnp.float32) + sign_row[...] * back).astype(jnp.bfloat16)
    for copy in started:
        copy.wait_send()


def vmem(shape, dtype):
    return pltpu.VMEM(shape, dtype)


def shards(resid, norm_gain, signs, query_weight, kv_weight, out_weight, lengths):
    bf16, f32 = jnp.bfloat16, jnp.float32
    dma = pltpu.SemaphoreType.DMA
    in_vmem = pl.BlockSpec(memory_space=pltpu.VMEM)
    in_any = pl.BlockSpec(memory_space=pl.ANY)
    order = token_order()
    inverse = np.exp(np.arange(HD // 2) * (-2.0 * math.log(rope_base) / HD))
    angles = inverse[:, None] * order[None, :]
    tok_cos = jnp.asarray(np.cos(angles), f32)
    tok_sin = jnp.asarray(np.sin(angles), f32)
    offsets = (jnp.cumsum(lengths) - lengths).astype(f32)
    off_angles = offsets[:, None] * jnp.asarray(inverse, f32)[None, :]
    off_cos = jnp.cos(off_angles)[:, :, None]
    off_sin = jnp.sin(off_angles)[:, :, None]
    here_section = lax.axis_index("section")
    oc = lax.dynamic_index_in_dim(off_cos, here_section, 0, keepdims=False)
    os = lax.dynamic_index_in_dim(off_sin, here_section, 0, keepdims=False)
    cosine = oc * tok_cos - os * tok_sin
    sine = os * tok_cos + oc * tok_sin
    had = hadamard(HB)
    had3 = jnp.asarray(np.concatenate([had, had, had], axis=0), bf16)
    sign_row = (2 * signs - 1).astype(f32)[None, :]
    gain_sign = norm_gain[None, :] * sign_row

    queries, kv = pl.pallas_call(
        project_kernel,
        out_shape=(
            jax.ShapeDtypeStruct((QC, TOK), bf16),
            jax.ShapeDtypeStruct((KC, TOK), bf16),
        ),
        in_specs=[in_vmem, in_vmem, in_vmem, in_any, in_any, in_vmem, in_vmem],
        out_specs=(in_vmem, in_vmem),
        scratch_shapes=[
            vmem((D, QC), bf16),
            vmem((D, KC), bf16),
            vmem((2, 4, NC, PR, SW), bf16),
            vmem((2, 4, NC, PR, CW), bf16),
            vmem((TOK, QC), f32),
            vmem((TOK, KC), f32),
            dma((2,)),
            dma((NC,)),
            dma((NC,)),
            dma((2, 3, NC)),
            dma((2, 3, NC)),
            dma((2, 3, NC)),
            dma((2, 3, NC)),
        ],
        compiler_params=pltpu.CompilerParams(
            collective_id=1, has_side_effects=True, vmem_limit_bytes=40 << 20
        ),
        name="project",
    )(resid, gain_sign, had3, query_weight, kv_weight, cosine, sine)

    key_tok = jnp.asarray(order[:, None], jnp.int32)
    query_tok = jnp.asarray(np.concatenate([order, order])[None, :], jnp.int32)
    return pl.pallas_call(
        attend_kernel,
        out_shape=jax.ShapeDtypeStruct(resid.shape, bf16),
        in_specs=[pl.BlockSpec(memory_space=pltpu.SMEM)]
        + [in_vmem] * 8
        + [in_any]
        + [in_vmem] * 3,
        out_specs=in_vmem,
        scratch_shapes=[
            vmem((QC, D), bf16),
            vmem((2, 2, 8, KC, TOK), bf16),
            vmem((TOK, QC), bf16),
            vmem((2, 4, NC, PR, CW), bf16),
            vmem((2, NC, PR, CW), bf16),
            vmem((2, 2, NC, PR, CW), bf16),
            vmem((2, 4, NC, PR, SW), bf16),
            vmem((2, NC, PR, SW), bf16),
            vmem((2, 2, NC, PR, SW), bf16),
            vmem((2, NC, PR, SW), f32),
            vmem((2, NC, PR, SW), bf16),
            vmem((NC, PR, SW), bf16),
            vmem((HD, 2 * TOK), f32),
            dma,
            dma,
            dma,
            dma((2, 4, 2)),
            dma((2, 4, 2)),
            dma((2, 8)),
            dma((2, 8)),
            dma((2, 3, NC)),
            dma((2, 3, NC)),
            dma((2, 3, NC)),
            dma((2, 3, NC)),
            dma((NC,)),
            dma((NC,)),
        ],
        compiler_params=pltpu.CompilerParams(
            collective_id=2, has_side_effects=True, vmem_limit_bytes=50 << 20
        ),
        name="attend",
    )(
        lengths, queries, kv, off_cos, off_sin, tok_cos, tok_sin, key_tok, query_tok,
        out_weight, resid, sign_row, had3,
    )


def solution(mesh):
    return jax.shard_map(
        shards,
        mesh=mesh,
        in_specs=(
            P("section", "tensor", None),
            P(),
            P(),
            P(None, "tensor"),
            P(None, "tensor"),
            P("tensor", None),
            P(),
        ),
        out_specs=P("section", "tensor", None),
        check_vma=False,
    )
```

```python
import functools
import math

import jax
import jax.numpy as jnp
import numpy as np
from jax import lax
from jax.experimental import pallas as pl
from jax.experimental.pallas import tpu as pltpu
from jax.sharding import PartitionSpec as P

MESH = pl.DeviceIdType.MESH
D = 8192
HD = 128
HB = 128
ROWS = 12
TOK = 384
BLOCKS = 8
NC = 4
HALF = D // 2
CW = HALF // NC
SUB = 4
SW = CW // SUB
PR = SUB * ROWS
QC = 256
KC = 64
rope_base = 500000.0
norm_eps = 1e-05
NEG = -1e30


def hadamard(extent):
    index = np.arange(extent)
    bits = index[:, None] & index[None, :]
    parity = np.zeros((extent, extent), np.int64)
    while bits.any():
        parity += bits & 1
        bits = bits >> 1
    return (1 - 2 * (parity % 2)).astype(np.float32)


def token_order():
    order = []
    for half in range(2):
        for j in range(4):
            for i in range(4):
                y, x = (j, i) if half == 0 else (i, j)
                t = (y * 4 + x) * 2 + half
                order.extend(range(t * ROWS, (t + 1) * ROWS))
    return np.array(order)


def here():
    t = lax.axis_index("tensor")
    s = lax.axis_index("section")
    y = t // 8
    x = lax.rem(t // 2, 4)
    z = (s // 2) * 2 + lax.rem(t, 2)
    return y, x, z, lax.rem(s, 2)


def device(y, x, z, c):
    return ((y * 4 + x) * 2 + lax.rem(z, 2), (z // 2) * 2 + c)


def shift(value, by, size):
    return lax.rem(value + (by + size), size)


def split3(value):
    high = value.astype(jnp.bfloat16)
    rest = value - high.astype(jnp.float32)
    middle = rest.astype(jnp.bfloat16)
    low = (rest - middle.astype(jnp.float32)).astype(jnp.bfloat16)
    return jnp.concatenate([high, middle, low], axis=1)


def greet(partners):
    barrier = pltpu.get_barrier_semaphore()
    for partner in partners:
        pl.semaphore_signal(barrier, inc=1, device_id=partner, device_id_type=MESH)
    pl.semaphore_wait(barrier, len(partners))


def remote(src, dst, send, recv, target):
    return pltpu.make_async_remote_copy(
        src_ref=src,
        dst_ref=dst,
        send_sem=send,
        recv_sem=recv,
        device_id=target,
        device_id_type=MESH,
    )


def sublayer_kernel(
    lengths, resid, gain, signs, had, inverse, tok_cos, tok_sin, key_tok, query_tok,
    q_hbm, kv_hbm, out_hbm, mixed,
    wq, wkv, wo, rot, p2, blocks, acc_q, acc_kv, cross, crossed, queries, off_cos, off_sin,
    kvs, top_ref, total_ref, acc, att, parts, raw1, fin1, parts2, raw2, fin2, sums, sums_bf, last_z, full,
    w_sem, swq, rwq, swo, rwo, sa, ra, sg2, rg2, sg3, rg3, scr, rcr, sx, rx, skv, rkv, sc, rc,
    sat, rat, s1, r1, s2, r2, sz, rz,
):
    y, x, z, core = here()
    low = lax.rem(z, 2)
    high = z // 2
    section = lax.axis_index("section")
    toward = 1 - 2 * low

    def at_x(by):
        return device(y, shift(x, by, 4), z, core)

    def at_y(by):
        return device(shift(y, by, 4), x, z, core)

    def at_z(by):
        return device(y, x, shift(z, by, 8), core)

    mate = at_z(toward)
    other_core = device(y, x, z, 1 - core)
    own_x = lax.rem(x, 2)
    x_mate = device(y, x + 1 - 2 * own_x, z, core)

    def ring_x(h, by):
        return device(shift(y, by * h, 4), shift(x, by * (1 - h), 4), z, core)

    def ring_y(h, by):
        return device(shift(y, by * (1 - h), 4), shift(x, by * h, 4), z, core)

    def pos_x(h):
        return x * (1 - h) + y * h

    def pos_y(h):
        return y * (1 - h) + x * h

    started = []

    def go(copy):
        copy.start()
        started.append(copy)

    greet([at_z(1), at_z(-1), other_core, at_x(1), at_x(-1), at_y(1), at_y(-1)])

    mine = pl.multiple_of(low * HALF, HALF)
    loads = [
        pltpu.make_async_copy(q_hbm.at[pl.ds(mine, HALF)], wq.at[0], w_sem.at[0]),
        pltpu.make_async_copy(kv_hbm.at[:, pl.ds(mine, HALF)], wkv.at[0], w_sem.at[1]),
        pltpu.make_async_copy(out_hbm.at[:, pl.ds(mine, HALF)], wo.at[0], w_sem.at[2]),
    ]
    QTR = HALF // 4

    def quarter(way, c):
        return (way * 2 + c) * QTR

    def ship_proj(way):
        target = at_z(toward * (1 - 2 * way))
        off = quarter(way, core)
        from_ = pl.multiple_of((1 - low) * HALF + off, QTR)
        to = pl.multiple_of(off, QTR)
        go(remote(q_hbm.at[pl.ds(from_, QTR)], wq.at[1, pl.ds(to, QTR)], swq.at[way, 0], rwq.at[way, 0], target))
        go(remote(kv_hbm.at[:, pl.ds(from_, QTR)], wkv.at[1, :, pl.ds(to, QTR)], swq.at[way, 1], rwq.at[way, 1], target))

    def share_proj(way):
        to = pl.multiple_of(quarter(way, core), QTR)
        q_ref, kv_ref = wq.at[1, pl.ds(to, QTR)], wkv.at[1, :, pl.ds(to, QTR)]
        remote(q_ref, q_ref, swq.at[way, 0], rwq.at[way, 0], mate).wait_recv()
        remote(kv_ref, kv_ref, swq.at[way, 1], rwq.at[way, 1], mate).wait_recv()
        go(remote(q_ref, q_ref, swq.at[2 + way, 0], rwq.at[2 + way, 0], other_core))
        go(remote(kv_ref, kv_ref, swq.at[2 + way, 1], rwq.at[2 + way, 1], other_core))

    def shared_proj(way):
        to = pl.multiple_of(quarter(way, 1 - core), QTR)
        q_ref, kv_ref = wq.at[1, pl.ds(to, QTR)], wkv.at[1, :, pl.ds(to, QTR)]
        remote(q_ref, q_ref, swq.at[2 + way, 0], rwq.at[2 + way, 0], other_core).wait_recv()
        remote(kv_ref, kv_ref, swq.at[2 + way, 1], rwq.at[2 + way, 1], other_core).wait_recv()

    def ship_out(way):
        target = at_z(toward * (1 - 2 * way))
        off = quarter(way, core)
        from_ = pl.multiple_of((1 - low) * HALF + off, QTR)
        to = pl.multiple_of(off, QTR)
        go(remote(out_hbm.at[:, pl.ds(from_, QTR)], wo.at[1, :, pl.ds(to, QTR)], swo.at[way], rwo.at[way], target))

    def share_out(way):
        ref = wo.at[1, :, pl.ds(pl.multiple_of(quarter(way, core), QTR), QTR)]
        remote(ref, ref, swo.at[way], rwo.at[way], mate).wait_recv()
        go(remote(ref, ref, swo.at[2 + way], rwo.at[2 + way], other_core))

    def shared_out(way):
        ref = wo.at[1, :, pl.ds(pl.multiple_of(quarter(way, 1 - core), QTR), QTR)]
        remote(ref, ref, swo.at[2 + way], rwo.at[2 + way], other_core).wait_recv()

    ship_proj(1)
    for load in loads:
        load.start()

    stream = resid[0].astype(jnp.float32)
    sign_row = (2 * signs[...] - 1).astype(jnp.float32)
    normed = (
        stream
        * lax.rsqrt(jnp.mean(stream * stream, axis=-1, keepdims=True) + norm_eps)
        * gain[...]
        * sign_row
    )
    per = SW // HB
    stacked = []
    for g in range(2 * NC):
        for b in range(per):
            stacked.append(
                jnp.concatenate(
                    [
                        normed[:, g * CW + j * SW + b * HB : g * CW + j * SW + (b + 1) * HB]
                        for j in range(SUB)
                    ],
                    axis=0,
                )
            )
    rotated = jnp.dot(
        split3(jnp.concatenate(stacked, axis=0)), had[...], preferred_element_type=jnp.float32
    ) * (1.0 / math.sqrt(HB))
    for g in range(2 * NC):
        blocks_of = [rotated[(g * per + b) * PR : (g * per + b + 1) * PR] for b in range(per)]
        rot[g // NC, g % NC] = jnp.concatenate(blocks_of, axis=1).astype(jnp.bfloat16)

    def swap_copy(c, h):
        return remote(
            rot.at[1 - low, c], p2.at[h, pos_x(h), c], sa.at[c], ra.at[c], mate
        )

    def direct(buf, pos, ssem, rsem, peer, h, c):
        ref = buf.at[h, pos(h), c]
        go(remote(ref, ref, ssem.at[h, 0, c], rsem.at[h, 0, c], peer(h, 1)))
        go(remote(ref, ref, ssem.at[h, 1, c], rsem.at[h, 1, c], peer(h, -1)))

    def arrive(buf, pos, ssem, rsem, peer, h, c):
        for kind, by in ((0, -1), (1, 1)):
            ref = buf.at[h, shift(pos(h), by, 4), c]
            remote(ref, ref, ssem.at[h, kind, c], rsem.at[h, kind, c], peer(h, 1)).wait_recv()
        by = -1 if c % 2 == 0 else 1
        ref = buf.at[h, shift(pos(h), by, 4), c]
        go(remote(ref, ref, ssem.at[h, 2, c], rsem.at[h, 2, c], peer(h, -by)))

    def last(buf, pos, ssem, rsem, peer, h, c):
        ref = buf.at[h, shift(pos(h), 2, 4), c]
        remote(ref, ref, ssem.at[h, 2, c], rsem.at[h, 2, c], peer(h, 1)).wait_recv()

    gather2 = (p2, pos_x, sg2, rg2, ring_x)
    gather3 = (blocks, pos_y, sg3, rg3, ring_y)
    for c in range(NC):
        go(swap_copy(c, low))
        p2[low, pos_x(low), c] = rot[low, c]
        direct(*gather2, low, c)
    ship_proj(0)
    for way in (1, 0):
        ship_out(way)
    for c in range(NC):
        swap_copy(c, 1 - low).wait_recv()
        direct(*gather2, 1 - low, c)
    for c in range(NC + 1):
        if c < NC:
            for h in range(2):
                arrive(*gather2, h, c)
        if c > 0:
            for h in range(2):
                last(*gather2, h, c - 1)
                pieces = [p2[h, i, c - 1].astype(jnp.float32) for i in range(4)]
                joined = jnp.concatenate(
                    [
                        jnp.concatenate(
                            [piece[j * ROWS : (j + 1) * ROWS] for piece in pieces], axis=0
                        )
                        for j in range(SUB)
                    ],
                    axis=1,
                )
                blocks[h, pos_y(h), c - 1] = joined.astype(jnp.bfloat16)
                direct(*gather3, h, c - 1)
    for load in loads:
        load.wait()

    def add_q(kind, c):
        part = jnp.dot(
            blocks[:, :, c].reshape(TOK, CW),
            wq[kind, c * CW : (c + 1) * CW],
            preferred_element_type=jnp.float32,
        )
        acc_q[kind] = part if c == 0 else acc_q[kind] + part

    def add_kv(c):
        part = lax.dot_general(
            blocks[:, :, c].reshape(TOK, CW),
            wkv[:, :, c * CW : (c + 1) * CW].reshape(2 * KC, CW),
            (((1,), (1,)), ((), ())),
            preferred_element_type=jnp.float32,
        )
        acc_kv[...] = part if c == 0 else acc_kv[...] + part

    lane = lax.broadcasted_iota(jnp.int32, (1, HB), 1)
    starts = jnp.zeros((1, HB), jnp.int32)
    for b in range(BLOCKS - 1):
        starts = starts + jnp.where(lane > b, lengths[b], 0)
    angles = inverse[...] * starts.astype(jnp.float32)
    off_cos[...] = jnp.cos(angles)
    off_sin[...] = jnp.sin(angles)

    def rotary_table(index):
        here_only = lane == index
        oc = jnp.sum(jnp.where(here_only, off_cos[...], 0.0), axis=1, keepdims=True)
        os = jnp.sum(jnp.where(here_only, off_sin[...], 0.0), axis=1, keepdims=True)
        return oc * tok_cos[...] - os * tok_sin[...], os * tok_cos[...] + oc * tok_sin[...]

    for c in range(NC):
        for h in range(2):
            arrive(*gather3, h, c)
        if c > 0:
            for h in range(2):
                last(*gather3, h, c - 1)
            if c < NC - 1:
                add_q(0, c - 1)
        if c == 1:
            share_proj(1)
        if c == 2:
            share_proj(0)
    for way in range(2):
        shared_proj(way)
    for c in range(NC - 1):
        add_kv(c)
        add_q(1, c)
    add_q(0, NC - 2)
    for h in range(2):
        last(*gather3, h, NC - 1)
    half = HD // 2

    def cross_copy(k):
        rows = pl.ds(0, KC) if k == 0 else pl.ds(KC, QC)
        return remote(cross.at[rows], crossed.at[rows], scr.at[k], rcr.at[k], mate)

    add_kv(NC - 1)
    kv_sum = jnp.transpose(acc_kv[...])
    cross[:KC] = kv_sum[KC:].astype(jnp.bfloat16)
    go(cross_copy(0))
    add_q(1, NC - 1)
    cross[KC:] = jnp.transpose(acc_q[1]).astype(jnp.bfloat16)
    go(cross_copy(1))

    def side(e):
        return own_x if e == 0 else 1 - own_x

    def hop(e, src_by, kind, dist, target):
        ref = kvs.at[core, side(e), shift(z, src_by, 8)]
        return remote(ref, ref, skv.at[kind, dist, e], rkv.at[kind, dist, e], target)

    def core_copy(e, k):
        ref = kvs.at[core, side(e), lax.rem(z + k, 8)]
        return remote(ref, ref, sc.at[e, k], rc.at[e, k], other_core)

    cross_copy(0).wait_recv()
    kvs[core, own_x, z] = (kv_sum[:KC] + crossed[:KC].astype(jnp.float32)).astype(jnp.bfloat16)
    own = kvs.at[core, own_x, z]
    go(remote(own, own, sx, rx, x_mate))
    go(hop(0, 0, 0, 0, at_z(1)))
    go(hop(0, 0, 1, 0, at_z(-1)))
    go(core_copy(0, 0))
    add_q(0, NC - 1)
    theirs = kvs.at[core, 1 - own_x, z]
    remote(theirs, theirs, sx, rx, x_mate).wait_recv()
    go(hop(1, 0, 0, 0, at_z(1)))
    go(hop(1, 0, 1, 0, at_z(-1)))
    go(core_copy(1, 0))

    cross_copy(1).wait_recv()
    turned = jnp.transpose(acc_q[0]) + crossed[KC:].astype(jnp.float32)
    cosine, sine = rotary_table(section)
    for head in range(2):
        first = turned[head * HD : head * HD + half]
        second = turned[head * HD + half : (head + 1) * HD]
        queries[:half, head * TOK : (head + 1) * TOK] = (
            first * cosine - second * sine
        ).astype(jnp.bfloat16)
        queries[half:, head * TOK : (head + 1) * TOK] = (
            second * cosine + first * sine
        ).astype(jnp.bfloat16)

    def ring_step(dist):
        for e in range(2):
            for kind, sgn in ((0, -1), (1, 1)):
                if dist == 3 and kind != e:
                    continue
                by = sgn * (dist + 1)
                hop(e, by, kind, dist, mate).wait_recv()
                if dist < 2 or (dist == 2 and kind == e):
                    go(hop(e, by, kind, dist + 1, at_z(-sgn)))
                go(core_copy(e, by % 8))

    def from_core(back):
        for u in range(2):
            k = shift(u - low, -2 * back + 8, 8)
            for e in range(2):
                ref = kvs.at[1 - core, side(e), lax.rem(z + k, 8)]
                remote(ref, ref, sc.at[e, k], rc.at[e, k], other_core).wait_recv()

    scale = math.log2(math.e) / math.sqrt(HD)

    def absorb(c, row, diagonal):
        index = row * 2 + c
        pair = pl.ds(row * 2, 2)
        raw = kvs[c, 0, pair].astype(jnp.float32)
        value = kvs[c, 1, pair].reshape(HD, TOK)
        cosine, sine = rotary_table(index)
        key = jnp.concatenate(
            [raw[0] * cosine - raw[1] * sine, raw[1] * cosine + raw[0] * sine], axis=0
        )
        key = jnp.transpose(key).astype(jnp.bfloat16)
        scores = jnp.dot(key, queries[...], preferred_element_type=jnp.float32)
        valid = key_tok[...] < lengths[index]
        if diagonal:
            seen = valid & (key_tok[...] <= query_tok[...])
            scores = jnp.where(seen, scores, NEG)
            top = jnp.max(scores, axis=0, keepdims=True)
            weights = jnp.exp2((scores - top) * scale)
            total_ref[...] = jnp.sum(weights, axis=0, keepdims=True)
            acc[...] = jnp.dot(
                value, weights.astype(jnp.bfloat16), preferred_element_type=jnp.float32
            )
        else:
            scores = scores + jnp.where(valid, 0.0, NEG)
            old = top_ref[...]
            top = jnp.maximum(old, jnp.max(scores, axis=0, keepdims=True))
            weights = jnp.exp2((scores - top) * scale)
            fade = jnp.exp2((old - top) * scale)
            total_ref[...] = total_ref[...] * fade + jnp.sum(weights, axis=0, keepdims=True)
            acc[...] = acc[...] * fade + jnp.dot(
                value, weights.astype(jnp.bfloat16), preferred_element_type=jnp.float32
            )
        top_ref[...] = top

    def earlier(back):
        @pl.when(high >= back)
        def _():
            for c in range(2):
                absorb(c, high - back, False)

    ring_step(0)
    from_core(0)
    absorb(core, high, True)

    @pl.when(core == 1)
    def _():
        absorb(0, high, False)

    ring_step(1)
    ring_step(2)
    from_core(1)
    from_core(3)
    earlier(1)
    earlier(3)
    ring_step(3)
    from_core(2)
    for way in range(2):
        share_out(way)
    earlier(2)
    attended = acc[...] / total_ref[...]
    for head in range(2):
        att[0, :, head * HD : (head + 1) * HD] = jnp.transpose(
            attended[:, head * TOK : (head + 1) * TOK]
        ).astype(jnp.bfloat16)
    att_copy = remote(att.at[0], att.at[1], sat, rat, mate)
    go(att_copy)
    for way in range(2):
        shared_out(way)
    att_copy.wait_recv()

    def send_raw(buf, raw, fin, pos, ssem, rsem, peer, h, c):
        by = 1 if c % 2 == 0 else -1
        go(
            remote(
                buf.at[h, shift(pos(h), 2, 4), c], raw.at[h, c], ssem.at[h, 2, c],
                rsem.at[h, 2, c], peer(h, by),
            )
        )

    def send_fin(buf, raw, fin, pos, ssem, rsem, peer, h, c, kind):
        by = 1 if kind == 0 else -1
        go(
            remote(
                buf.at[h, shift(pos(h), by, 4), c], fin.at[h, kind, c], ssem.at[h, kind, c],
                rsem.at[h, kind, c], peer(h, by),
            )
        )

    def pass_on(buf, raw, fin, pos, ssem, rsem, peer, h, c):
        kind, by = (0, 1) if c % 2 == 0 else (1, -1)
        ref = raw.at[h, c]
        remote(ref, ref, ssem.at[h, 2, c], rsem.at[h, 2, c], peer(h, 1)).wait_recv()
        slot = shift(pos(h), by, 4)
        buf[h, slot, c] = (
            buf[h, slot, c].astype(jnp.float32) + raw[h, c].astype(jnp.float32)
        ).astype(jnp.bfloat16)
        send_fin(buf, raw, fin, pos, ssem, rsem, peer, h, c, kind)

    def finish(buf, raw, fin, pos, ssem, rsem, peer, h, c):
        for kind in range(2):
            ref = fin.at[h, kind, c]
            remote(ref, ref, ssem.at[h, kind, c], rsem.at[h, kind, c], peer(h, 1)).wait_recv()
        return (
            buf[h, pos(h), c].astype(jnp.float32)
            + fin[h, 0, c].astype(jnp.float32)
            + fin[h, 1, c].astype(jnp.float32)
        )

    ring1 = (parts, raw1, fin1, pos_y, s1, r1, ring_y)
    ring2 = (parts2, raw2, fin2, pos_x, s2, r2, ring_x)
    for c in range(NC):
        columns = pl.ds(c * CW, CW)
        partial = jnp.dot(
            att[0], wo[0, :, columns], preferred_element_type=jnp.float32
        ) + jnp.dot(att[1], wo[1, :, columns], preferred_element_type=jnp.float32)
        parts[:, :, c] = partial.astype(jnp.bfloat16).reshape(2, 4, PR, CW)
        for h in range(2):
            send_raw(*ring1, h, c)
            send_fin(*ring1, h, c, 1 if c % 2 == 0 else 0)
    for c in range(NC):
        for h in range(2):
            pass_on(*ring1, h, c)

    def z_copy(c, h):
        return remote(sums_bf.at[h, c], last_z.at[c], sz.at[c], rz.at[c], mate)

    for c in range(NC + 2):
        if c < NC:
            for h in range(2):
                done = finish(*ring1, h, c)
                for i in range(4):
                    parts2[h, i, c] = jnp.concatenate(
                        [
                            done[i * ROWS : (i + 1) * ROWS, j * SW : (j + 1) * SW]
                            for j in range(SUB)
                        ],
                        axis=0,
                    ).astype(jnp.bfloat16)
                send_raw(*ring2, h, c)
                send_fin(*ring2, h, c, 1 if c % 2 == 0 else 0)
        if 0 < c <= NC:
            for h in range(2):
                pass_on(*ring2, h, c - 1)
        if c > 1:
            for h in range(2):
                done = finish(*ring2, h, c - 2)
                sums[h, c - 2] = done
                sums_bf[h, c - 2] = done.astype(jnp.bfloat16)
            go(z_copy(c - 2, 1 - low))
    full[low] = sums[low]
    for c in range(NC):
        z_copy(c, low).wait_recv()
        full[1 - low, c] = last_z[c].astype(jnp.float32)
    stacked = []
    for g in range(2 * NC):
        branch = full[g // NC, g % NC]
        stacked += [branch[:, b * HB : (b + 1) * HB] for b in range(per)]
    back = jnp.dot(
        split3(jnp.concatenate(stacked, axis=0)), had[...], preferred_element_type=jnp.float32
    ) * (1.0 / math.sqrt(HB))
    columns = []
    for g in range(2 * NC):
        for j in range(SUB):
            for b in range(per):
                row = (g * per + b) * PR + j * ROWS
                columns.append(back[row : row + ROWS])
    back = jnp.concatenate(columns, axis=1)
    sign_row = (2 * signs[...] - 1).astype(jnp.float32)
    mixed[0] = (resid[0].astype(jnp.float32) + sign_row * back).astype(jnp.bfloat16)
    for copy in started:
        copy.wait_send()


def vmem(shape, dtype):
    return pltpu.VMEM(shape, dtype)


def shards(resid, norm_gain, signs, query_weight, kv_weight, out_weight, lengths):
    bf16, f32 = jnp.bfloat16, jnp.float32
    dma = pltpu.SemaphoreType.DMA
    in_vmem = pl.BlockSpec(memory_space=pltpu.VMEM)
    in_any = pl.BlockSpec(memory_space=pl.ANY)
    order = token_order()
    inverse = np.exp(np.arange(HD // 2) * (-2.0 * math.log(rope_base) / HD))
    angles = inverse[:, None] * order[None, :]
    had = hadamard(HB)
    ring = dma((2, 3, NC))
    return pl.pallas_call(
        sublayer_kernel,
        out_shape=jax.ShapeDtypeStruct(resid.shape, bf16),
        in_specs=[pl.BlockSpec(memory_space=pltpu.SMEM)] + [in_vmem] * 9 + [in_any] * 3,
        out_specs=in_vmem,
        scratch_shapes=[
            vmem((2, HALF, QC), bf16),
            vmem((2, KC, HALF), bf16),
            vmem((2, QC, HALF), bf16),
            vmem((2, NC, PR, SW), bf16),
            vmem((2, 4, NC, PR, SW), bf16),
            vmem((2, 4, NC, PR, CW), bf16),
            vmem((2, TOK, QC), f32),
            vmem((TOK, 2 * KC), f32),
            vmem((KC + QC, TOK), bf16),
            vmem((KC + QC, TOK), bf16),
            vmem((HD, 2 * TOK), bf16),
            vmem((HD // 2, HB), f32),
            vmem((HD // 2, HB), f32),
            vmem((2, 2, 8, KC, TOK), bf16),
            vmem((1, 2 * TOK), f32),
            vmem((1, 2 * TOK), f32),
            vmem((HD, 2 * TOK), f32),
            vmem((2, TOK, QC), bf16),
            vmem((2, 4, NC, PR, CW), bf16),
            vmem((2, NC, PR, CW), bf16),
            vmem((2, 2, NC, PR, CW), bf16),
            vmem((2, 4, NC, PR, SW), bf16),
            vmem((2, NC, PR, SW), bf16),
            vmem((2, 2, NC, PR, SW), bf16),
            vmem((2, NC, PR, SW), f32),
            vmem((2, NC, PR, SW), bf16),
            vmem((NC, PR, SW), bf16),
            vmem((2, NC, PR, SW), f32),
            dma((3,)),
            dma((4, 2)),
            dma((4, 2)),
            dma((4,)),
            dma((4,)),
            dma((NC,)),
            dma((NC,)),
            ring,
            ring,
            ring,
            ring,
            dma((2,)),
            dma((2,)),
            dma,
            dma,
            dma((2, 4, 2)),
            dma((2, 4, 2)),
            dma((2, 8)),
            dma((2, 8)),
            dma,
            dma,
            ring,
            ring,
            ring,
            ring,
            dma((NC,)),
            dma((NC,)),
        ],
        compiler_params=pltpu.CompilerParams(
            collective_id=1, has_side_effects=True, vmem_limit_bytes=50 << 20
        ),
        name="sublayer",
    )(
        lengths, resid, norm_gain[None, :], signs[None, :],
        jnp.asarray(np.concatenate([had, had, had], axis=0), bf16),
        jnp.asarray(inverse[:, None], f32),
        jnp.asarray(np.cos(angles), f32), jnp.asarray(np.sin(angles), f32),
        jnp.asarray(order[:, None], jnp.int32),
        jnp.asarray(np.concatenate([order, order])[None, :], jnp.int32),
        query_weight, kv_weight.T, out_weight,
    )


def solution(mesh):
    return jax.shard_map(
        shards,
        mesh=mesh,
        in_specs=(
            P("section", "tensor", None),
            P(),
            P(),
            P(None, "tensor"),
            P(None, "tensor"),
            P("tensor", None),
            P(),
        ),
        out_specs=P("section", "tensor", None),
        check_vma=False,
    )
```

```python
import functools
import math

import jax
import jax.numpy as jnp
import numpy as np
from jax import lax
from jax.experimental import pallas as pl
from jax.experimental.pallas import tpu as pltpu
from jax.sharding import PartitionSpec as P

MESH = pl.DeviceIdType.MESH
D = 8192
HD = 128
HB = 128
ROWS = 12
TOK = 384
BLOCKS = 8
NC = 4
HALF = D // 2
CW = HALF // NC
SUB = 4
SW = CW // SUB
PR = SUB * ROWS
QC = 256
KC = 64
rope_base = 500000.0
norm_eps = 1e-05
NEG = -1e30


def token_order():
    order = []
    for half in range(2):
        for i in range(4):
            for j in range(4):
                y, x = (j, i) if half == 0 else (i, j)
                t = (y * 4 + x) * 2 + half
                order.extend(range(t * ROWS, (t + 1) * ROWS))
    return np.array(order)


def here():
    t = lax.axis_index("tensor")
    s = lax.axis_index("section")
    y = t // 8
    x = lax.rem(t // 2, 4)
    z = (s // 2) * 2 + lax.rem(t, 2)
    return y, x, z, lax.rem(s, 2)


def device(y, x, z, c):
    return ((y * 4 + x) * 2 + lax.rem(z, 2), (z // 2) * 2 + c)


def shift(value, by, size):
    return lax.rem(value + (by + size), size)


def split3(value):
    high = value.astype(jnp.bfloat16)
    rest = value - high.astype(jnp.float32)
    middle = rest.astype(jnp.bfloat16)
    low = (rest - middle.astype(jnp.float32)).astype(jnp.bfloat16)
    return jnp.concatenate([high, middle, low], axis=1)


def greet(partners):
    barrier = pltpu.get_barrier_semaphore()
    for partner in partners:
        pl.semaphore_signal(barrier, inc=1, device_id=partner, device_id_type=MESH)


def met(partners):
    pl.semaphore_wait(pltpu.get_barrier_semaphore(), len(partners))


def remote(src, dst, send, recv, target):
    return pltpu.make_async_remote_copy(
        src_ref=src,
        dst_ref=dst,
        send_sem=send,
        recv_sem=recv,
        device_id=target,
        device_id_type=MESH,
    )


def sublayer_kernel(
    lengths_hbm, resid_hbm, gain_hbm, signs_hbm, table_hbm, q_hbm, kv_hbm, out_hbm, mixed,
    lengths, resid, gain, signs, table, had, key_tok, wq, wkv, wo, rot, pieces, rows_ref, acc_q, acc_kv, cross_q, cross_kv, crossed_q, crossed_kv, queries, off_cos, off_sin,
    kvs, top_ref, total_ref, acc, att, parts, raw1, fin1, parts2, fin2, full,
    in_sem, w_sem, swq, rwq, swo, rwo, sa, ra, sg2, rg2, sg3, rg3, scr, rcr, sx, rx, skv, rkv, sc, rc,
    sat, rat, s1, r1, s2, r2,
):
    y, x, z, core = here()
    low = lax.rem(z, 2)
    high = z // 2
    section = lax.axis_index("section")
    toward = 1 - 2 * low

    def at_x(by):
        return device(y, shift(x, by, 4), z, core)

    def at_y(by):
        return device(shift(y, by, 4), x, z, core)

    def at_z(by):
        return device(y, x, shift(z, by, 8), core)

    mate = at_z(toward)
    other_core = device(y, x, z, 1 - core)
    own_x = lax.rem(x, 2)

    def x_mate_at(by):
        return device(y, x + 1 - 2 * own_x, shift(z, by, 8), core)

    x_mate = x_mate_at(0)

    def ring_x(h, by):
        return device(shift(y, by * h, 4), shift(x, by * (1 - h), 4), z, core)

    def ring_y(h, by):
        return device(shift(y, by * (1 - h), 4), shift(x, by * h, 4), z, core)

    def pos_x(h):
        return x * (1 - h) + y * h

    def pos_y(h):
        return y * (1 - h) + x * h

    started = []

    def go(copy):
        copy.start()
        started.append(copy)

    def beyond(by):
        h = 1 - low
        return device(shift(y, by * h, 4), shift(x, by * (1 - h), 4), shift(z, toward, 8), core)

    def behind(by):
        return device(
            shift(y, by * low, 4), shift(x, by * (1 - low), 4), shift(z, toward, 8), core
        )

    partners = [at_z(by) for by in (1, -1, 2, -2)] + [other_core]
    partners += [at_x(by) for by in (1, -1, 2)] + [at_y(by) for by in (1, -1, 2)]
    partners += [behind(by) for by in (1, -1, 2)]
    partners += [x_mate_at(by) for by in (1, -1, 2, -2)]
    greet(partners)
    inputs = [
        pltpu.make_async_copy(from_, to, in_sem.at[k])
        for k, (from_, to) in enumerate(
            [
                (resid_hbm, resid), (gain_hbm, gain), (signs_hbm, signs), (lengths_hbm, lengths),
                (table_hbm, table),
            ]
        )
    ]
    for copy in inputs:
        copy.start()

    mine = pl.multiple_of(low * HALF, HALF)
    loads = [
        pltpu.make_async_copy(q_hbm.at[pl.ds(mine, HALF)], wq.at[0], w_sem.at[0]),
        pltpu.make_async_copy(kv_hbm.at[:, pl.ds(mine, HALF)], wkv.at[0], w_sem.at[1]),
        pltpu.make_async_copy(out_hbm.at[:, pl.ds(mine, HALF)], wo.at[0], w_sem.at[2]),
    ]
    QTR = HALF // 4

    def quarter(way, c):
        return (way * 2 + c) * QTR

    def ship_proj(way):
        target = at_z(toward * (1 - 2 * way))
        off = quarter(way, core)
        from_ = pl.multiple_of((1 - low) * HALF + off, QTR)
        to = pl.multiple_of(off, QTR)
        go(remote(q_hbm.at[pl.ds(from_, QTR)], wq.at[1, pl.ds(to, QTR)], swq.at[way, 0], rwq.at[way, 0], target))
        go(remote(kv_hbm.at[:, pl.ds(from_, QTR)], wkv.at[1, :, pl.ds(to, QTR)], swq.at[way, 1], rwq.at[way, 1], target))

    def share_proj(way):
        to = pl.multiple_of(quarter(way, core), QTR)
        q_ref, kv_ref = wq.at[1, pl.ds(to, QTR)], wkv.at[1, :, pl.ds(to, QTR)]
        remote(q_ref, q_ref, swq.at[way, 0], rwq.at[way, 0], mate).wait_recv()
        remote(kv_ref, kv_ref, swq.at[way, 1], rwq.at[way, 1], mate).wait_recv()
        go(remote(q_ref, q_ref, swq.at[2 + way, 0], rwq.at[2 + way, 0], other_core))
        go(remote(kv_ref, kv_ref, swq.at[2 + way, 1], rwq.at[2 + way, 1], other_core))

    def shared_proj(way):
        to = pl.multiple_of(quarter(way, 1 - core), QTR)
        q_ref, kv_ref = wq.at[1, pl.ds(to, QTR)], wkv.at[1, :, pl.ds(to, QTR)]
        remote(q_ref, q_ref, swq.at[2 + way, 0], rwq.at[2 + way, 0], other_core).wait_recv()
        remote(kv_ref, kv_ref, swq.at[2 + way, 1], rwq.at[2 + way, 1], other_core).wait_recv()

    def out_part(part, c):
        start = quarter(1, c) if part == 0 else quarter(0, c) + (part - 1) * (QTR // 2)
        return start, QTR if part == 0 else QTR // 2

    def ship_out(part):
        target = at_z(toward if part == 1 else -toward)
        start, width = out_part(part, core)
        from_ = pl.multiple_of((1 - low) * HALF + start, width)
        to = pl.multiple_of(start, width)
        go(remote(out_hbm.at[:, pl.ds(from_, width)], wo.at[1, :, pl.ds(to, width)], swo.at[part], rwo.at[part], target))

    def share_out(part):
        start, width = out_part(part, core)
        ref = wo.at[1, :, pl.ds(pl.multiple_of(start, width), width)]
        remote(ref, ref, swo.at[part], rwo.at[part], mate).wait_recv()
        go(remote(ref, ref, swo.at[3 + part], rwo.at[3 + part], other_core))

    def shared_out(part):
        start, width = out_part(part, 1 - core)
        ref = wo.at[1, :, pl.ds(pl.multiple_of(start, width), width)]
        remote(ref, ref, swo.at[3 + part], rwo.at[3 + part], other_core).wait_recv()

    for load in loads:
        load.start()
    row = lax.broadcasted_iota(jnp.int32, (HB, HB), 0)
    column = lax.broadcasted_iota(jnp.int32, (HB, HB), 1)
    odd = row & column
    for bits in (4, 2, 1):
        odd = odd ^ (odd >> bits)
    signed = (1 - 2 * (odd & 1)).astype(jnp.float32).astype(jnp.bfloat16)
    for k in range(3):
        had[k * HB : (k + 1) * HB] = signed
    for copy in inputs[:3]:
        copy.wait()

    stream = resid[0].astype(jnp.float32)
    sign_row = (2 * signs[...] - 1).astype(jnp.float32)
    normed = (
        stream
        * lax.rsqrt(jnp.mean(stream * stream, axis=-1, keepdims=True) + norm_eps)
        * gain[...]
        * sign_row
    )
    per = SW // HB
    stacked = []
    for g in range(2 * NC):
        for b in range(per):
            stacked.append(
                jnp.concatenate(
                    [
                        normed[:, g * CW + j * SW + b * HB : g * CW + j * SW + (b + 1) * HB]
                        for j in range(SUB)
                    ],
                    axis=0,
                )
            )
    rotated = jnp.dot(
        split3(jnp.concatenate(stacked, axis=0)), had[...], preferred_element_type=jnp.float32
    ) * (1.0 / math.sqrt(HB))
    for g in range(2 * NC):
        blocks_of = [rotated[(g * per + b) * PR : (g * per + b + 1) * PR] for b in range(per)]
        rot[g // NC, g % NC] = jnp.concatenate(blocks_of, axis=1).astype(jnp.bfloat16)

    met(partners)

    STEP = (0, -1, 1, 2)

    def piece(h, dj, di):
        return pieces.at[h, shift(pos_y(h), dj, 4), shift(pos_x(h), di, 4)]

    def swap_copy(h):
        return remote(rot.at[1 - low], piece(h, 0, 0), sa, ra, mate)

    def spread_x(h):
        ref = piece(h, 0, 0)
        for k in (1, 2, 3):
            go(remote(ref, ref, sg2.at[h, k - 1], rg2.at[h, k - 1], ring_x(h, -STEP[k])))

    def spread_y(h, k):
        ref = piece(h, 0, STEP[k])
        for kind, by in ((0, 1), (1, -1)):
            go(remote(ref, ref, sg3.at[h, kind, k], rg3.at[h, kind, k], ring_y(h, by)))

    def from_x(h, k):
        ref = piece(h, 0, STEP[k])
        remote(ref, ref, sg2.at[h, k - 1], rg2.at[h, k - 1], mate).wait_recv()

    def from_y(h, k):
        for kind, by in ((0, -1), (1, 1)):
            ref = piece(h, by, STEP[k])
            remote(ref, ref, sg3.at[h, kind, k], rg3.at[h, kind, k], mate).wait_recv()
        by = -1 if k in (0, 3) else 1
        ref = piece(h, by, STEP[k])
        go(remote(ref, ref, sg3.at[h, 2, k], rg3.at[h, 2, k], ring_y(h, -by)))

    def from_far(h, k):
        ref = piece(h, 2, STEP[k])
        remote(ref, ref, sg3.at[h, 2, k], rg3.at[h, 2, k], mate).wait_recv()

    pieces[low, pos_y(low), pos_x(low)] = rot[low]
    go(swap_copy(low))
    ship_proj(1)
    spread_x(low)
    spread_y(low, 0)
    ship_proj(0)
    swap_copy(1 - low).wait_recv()
    spread_x(1 - low)
    spread_y(1 - low, 0)
    high_half = 1 - low
    for k in (1, 2, 3):
        from_x(low, k)
        spread_y(low, k)
    from_y(low, 0)
    for k in (1, 2, 3):
        from_x(high_half, k)
        spread_y(high_half, k)
    from_y(low, 1)
    from_y(high_half, 0)
    ship_out(0)
    ship_out(2)
    from_y(low, 2)
    from_y(high_half, 1)
    for load in loads:
        load.wait()

    def join(k):
        for h in range(2):
            i = shift(pos_x(h), STEP[k], 4)
            for c in range(NC):
                parts_of = [pieces[h, j, i, c].astype(jnp.float32) for j in range(4)]
                rows_ref[k, h, :, c * CW : (c + 1) * CW] = jnp.concatenate(
                    [
                        jnp.concatenate(
                            [part[u * ROWS : (u + 1) * ROWS] for part in parts_of], axis=0
                        )
                        for u in range(SUB)
                    ],
                    axis=1,
                ).astype(jnp.bfloat16)

    def group(k):
        return rows_ref[k].reshape(2 * PR, HALF)

    def add_own():
        part = jnp.dot(
            rows_ref[...].reshape(8 * PR, HALF), wq[0], preferred_element_type=jnp.float32
        )
        for k in range(4):
            for h in range(2):
                start = (k * 2 + h) * PR
                acc_q[h, shift(pos_x(h), STEP[k], 4)] = part[start : start + PR]

    def add_mates(k):
        part = jnp.dot(group(k), wq[1], preferred_element_type=jnp.float32)
        for h in range(2):
            cross_q[h, shift(pos_x(h), STEP[k], 4)] = part[h * PR : (h + 1) * PR].astype(
                jnp.bfloat16
            )

    def add_kv(k):
        part = lax.dot_general(
            group(k),
            wkv[...].reshape(2 * KC, HALF),
            (((1,), (1,)), ((), ())),
            preferred_element_type=jnp.float32,
        )
        for h in range(2):
            i = shift(pos_x(h), STEP[k], 4)
            acc_kv[h, i] = part[h * PR : (h + 1) * PR]
            cross_kv[h, i] = part[h * PR : (h + 1) * PR].astype(jnp.bfloat16)

    def cross_copy(kind, h, k):
        i = shift(pos_x(h), STEP[k], 4)
        src, dst = ((cross_kv, crossed_kv), (cross_q, crossed_q))[kind]
        return remote(src.at[h, i], dst.at[h, i], scr.at[kind, h, k], rcr.at[kind, h, k], mate)

    def cross_group(k):
        add_kv(k)
        for h in range(2):
            go(cross_copy(0, h, k))
        add_mates(k)
        for h in range(2):
            go(cross_copy(1, h, k))

    for copy in inputs[3:]:
        copy.wait()
    tok_cos = table.at[: HD // 2, :TOK]
    tok_sin = table.at[: HD // 2, TOK : 2 * TOK]
    query_tok = table.at[HD // 2 : HD // 2 + 1, : 2 * TOK]
    inverse = table.at[: HD // 2, 2 * TOK :]
    key_tok[...] = jnp.transpose(
        jnp.broadcast_to(table[HD // 2 : HD // 2 + 1, :TOK], (HB, TOK))
    )
    lane = lax.broadcasted_iota(jnp.int32, (1, HB), 1)
    starts = jnp.zeros((1, HB), jnp.int32)
    for b in range(BLOCKS - 1):
        starts = starts + jnp.where(lane > b, lengths[b], 0)
    angles = inverse[...] * starts.astype(jnp.float32)
    off_cos[...] = jnp.cos(angles)
    off_sin[...] = jnp.sin(angles)

    def rotary_table(index):
        here_only = lane == index
        oc = jnp.sum(jnp.where(here_only, off_cos[...], 0.0), axis=1, keepdims=True)
        os = jnp.sum(jnp.where(here_only, off_sin[...], 0.0), axis=1, keepdims=True)
        return oc * tok_cos[...] - os * tok_sin[...], os * tok_cos[...] + oc * tok_sin[...]

    def own_group(k):
        for h in range(2):
            from_far(h, k)
        join(k)

    own_group(0)
    from_y(low, 3)
    from_y(high_half, 2)
    share_proj(1)
    share_proj(0)
    ship_out(1)
    own_group(1)
    for way in range(2):
        shared_proj(way)
    cross_group(0)
    from_y(high_half, 3)
    cross_group(1)
    own_group(2)
    cross_group(2)
    for h in range(2):
        from_far(h, 3)
    join(3)
    cross_group(3)
    half = HD // 2

    def side(e):
        return own_x if e == 0 else 1 - own_x

    def kv_piece(e, by):
        return kvs.at[core, side(e), shift(z, by, 8)]

    def along(by, hops, kind):
        ref = kv_piece(0, by)
        return remote(ref, ref, skv.at[kind], rkv.at[kind], at_z(hops))

    def across(by, hops, kind):
        ref = kv_piece(0, by)
        return remote(ref, ref, sx.at[kind], rx.at[kind], x_mate_at(hops))

    def to_mates(by, x_too=True):
        ref = kv_piece(0, by)
        k = by % 8
        if x_too:
            go(remote(ref, ref, sx.at[k], rx.at[k], x_mate))
        go(remote(ref, ref, sc.at[0, k], rc.at[0, k], other_core))

    def from_x_mate(by):
        ref = kv_piece(1, by)
        k = by % 8
        remote(ref, ref, sx.at[k], rx.at[k], x_mate).wait_recv()
        go(remote(ref, ref, sc.at[1, k], rc.at[1, k], other_core))

    for k in range(4):
        for h in range(2):
            cross_copy(0, h, k).wait_recv()
    kv_sum = acc_kv[...].reshape(TOK, 2 * KC) + pltpu.roll(
        crossed_kv[...].astype(jnp.float32).reshape(TOK, 2 * KC), KC, 1
    )
    kvs[core, own_x, z] = jnp.transpose(kv_sum)[:KC].astype(jnp.bfloat16)
    go(along(0, 2, 2))
    go(along(0, -2, 3))
    go(along(0, 1, 0))
    go(along(0, -1, 1))
    to_mates(0)
    add_own()

    for k in range(4):
        for h in range(2):
            cross_copy(1, h, k).wait_recv()
    turned = jnp.transpose(
        (acc_q[...] + crossed_q[...].astype(jnp.float32)).reshape(TOK, QC)
    )
    cosine, sine = rotary_table(section)
    for head in range(2):
        first = turned[head * HD : head * HD + half]
        second = turned[head * HD + half : (head + 1) * HD]
        queries[:half, head * TOK : (head + 1) * TOK] = (
            first * cosine - second * sine
        ).astype(jnp.bfloat16)
        queries[half:, head * TOK : (head + 1) * TOK] = (
            second * cosine + first * sine
        ).astype(jnp.bfloat16)

    def from_core(back):
        for u in range(2):
            k = shift(u - low, 8 - 2 * back, 8)
            for e in range(2):
                ref = kvs.at[1 - core, side(e), lax.rem(z + k, 8)]
                remote(ref, ref, sc.at[e, k], rc.at[e, k], other_core).wait_recv()

    scale = math.log2(math.e) / math.sqrt(HD)

    def absorb(c, row, diagonal):
        index = row * 2 + c
        pair = pl.ds(row * 2, 2)
        raw = kvs[c, 0, pair].astype(jnp.float32)
        value = kvs[c, 1, pair].reshape(HD, TOK)
        cosine, sine = rotary_table(index)
        key = jnp.concatenate(
            [raw[0] * cosine - raw[1] * sine, raw[1] * cosine + raw[0] * sine], axis=0
        )
        key = jnp.transpose(key).astype(jnp.bfloat16)
        scores = jnp.dot(key, queries[...], preferred_element_type=jnp.float32)
        token = key_tok[:, :1]
        valid = token < lengths[index].astype(jnp.float32)
        if diagonal:
            seen = valid & (token <= query_tok[...])
            scores = jnp.where(seen, scores, NEG)
            top = jnp.max(scores, axis=0, keepdims=True)
            weights = jnp.exp2((scores - top) * scale)
            total_ref[...] = jnp.sum(weights, axis=0, keepdims=True)
            acc[...] = jnp.dot(
                value, weights.astype(jnp.bfloat16), preferred_element_type=jnp.float32
            )
        else:
            scores = scores + jnp.where(valid, 0.0, NEG)
            old = top_ref[...]
            top = jnp.maximum(old, jnp.max(scores, axis=0, keepdims=True))
            weights = jnp.exp2((scores - top) * scale)
            fade = jnp.exp2((old - top) * scale)
            total_ref[...] = total_ref[...] * fade + jnp.sum(weights, axis=0, keepdims=True)
            acc[...] = acc[...] * fade + jnp.dot(
                value, weights.astype(jnp.bfloat16), preferred_element_type=jnp.float32
            )
        top_ref[...] = top

    def earlier(back):
        @pl.when(high >= back)
        def _():
            for c in range(2):
                absorb(c, high - back, False)

    for by, kind in ((-2, 2), (2, 3)):
        along(by, 0, kind).wait_recv()
        on = 1 if by < 0 else -1
        go(along(by, on, 4 if by < 0 else 5))
        go(across(by, on, (by - on) % 8))
        to_mates(by)
    turn = 2 - 4 * core
    go(along(-turn, turn, 6))
    go(across(-turn, turn, 4))
    for by, kind in ((-1, 0), (1, 1)):
        along(by, 0, kind).wait_recv()
        to_mates(by)
    for by in (0, -2, 2, -1, 1):
        from_x_mate(by)
    for by, kind in ((-3, 4), (3, 5), (4, 6)):
        along(by, 0, kind).wait_recv()
        to_mates(by, False)
    from_core(0)
    absorb(core, high, True)

    @pl.when(core == 1)
    def _():
        absorb(0, high, False)

    for part in range(3):
        share_out(part)
    for by in (-3, 3, 4):
        from_x_mate(by)
    near = 1 + 2 * low
    for back in (near, 4 - near, 2):
        from_core(back)
        earlier(back)
    attended = acc[...] / total_ref[...]
    for head in range(2):
        rows = jnp.transpose(attended[:, head * TOK : (head + 1) * TOK])
        for h in range(2):
            for j in range(4):
                att[0, h, j, :, head * HD : (head + 1) * HD] = jnp.concatenate(
                    [
                        rows[h * 4 * PR + i * PR + j * ROWS : h * 4 * PR + i * PR + (j + 1) * ROWS]
                        for i in range(4)
                    ],
                    axis=0,
                ).astype(jnp.bfloat16)
    def att_copy(h, k):
        j = shift(pos_y(h), FAR_FIRST[k], 4)
        return remote(att.at[0, h, j], att.at[1, h, j], sat.at[h, k], rat.at[h, k], mate)

    FAR_FIRST = (2, 1, -1, 0)
    for k in range(4):
        for h in range(2):
            go(att_copy(h, k))
    for part in range(3):
        shared_out(part)

    def send_raw(buf, raw, fin, pos, ssem, rsem, peer, h, c):
        by = 1 if c % 2 == 0 else -1
        go(
            remote(
                buf.at[h, shift(pos(h), 2, 4), c], raw.at[h, c], ssem.at[h, 2, c],
                rsem.at[h, 2, c], peer(h, by),
            )
        )

    def send_fin(buf, raw, fin, pos, ssem, rsem, peer, h, c, kind):
        by = 1 if kind == 0 else -1
        go(
            remote(
                buf.at[h, shift(pos(h), by, 4), c], fin.at[h, kind, c], ssem.at[h, kind, c],
                rsem.at[h, kind, c], peer(h, by),
            )
        )

    def pass_on(buf, raw, fin, pos, ssem, rsem, peer, h, c):
        kind, by = (0, 1) if c % 2 == 0 else (1, -1)
        ref = raw.at[h, c]
        remote(ref, ref, ssem.at[h, 2, c], rsem.at[h, 2, c], peer(h, 1)).wait_recv()
        slot = shift(pos(h), by, 4)
        buf[h, slot, c] = (
            buf[h, slot, c].astype(jnp.float32) + raw[h, c].astype(jnp.float32)
        ).astype(jnp.bfloat16)
        send_fin(buf, raw, fin, pos, ssem, rsem, peer, h, c, kind)

    def finish(buf, raw, fin, pos, ssem, rsem, peer, h, c):
        for kind in range(2):
            ref = fin.at[h, kind, c]
            remote(ref, ref, ssem.at[h, kind, c], rsem.at[h, kind, c], peer(h, 1)).wait_recv()
        return (
            buf[h, pos(h), c].astype(jnp.float32)
            + fin[h, 0, c].astype(jnp.float32)
            + fin[h, 1, c].astype(jnp.float32)
        )

    ring1 = (parts, raw1, fin1, pos_y, s1, r1, ring_y)

    def scatter_x(c):
        for k in range(4):
            i = shift(pos_x(low), -STEP[k], 4)
            j = shift(pos_x(1 - low), -STEP[k], 4)
            near_chip = ring_x(low, -STEP[k])
            far_chip = beyond(-STEP[k])
            if k > 0:
                go(
                    remote(
                        parts2.at[low, i, c], fin2.at[0, k, c], s2.at[0, k, c], r2.at[0, k, c], near_chip
                    )
                )
            go(
                remote(
                    parts2.at[1 - low, j, c], fin2.at[1, k, c], s2.at[1, k, c], r2.at[1, k, c], far_chip
                )
            )

    def sum_x(where, c):
        done = parts2[low, pos_x(low), c].astype(jnp.float32) if where == 0 else None
        for k in range(4):
            if where == 0 and k == 0:
                continue
            ref = fin2.at[where, k, c]
            remote(ref, ref, s2.at[where, k, c], r2.at[where, k, c], mate).wait_recv()
            term = fin2[where, k, c].astype(jnp.float32)
            done = term if done is None else done + term
        return done

    sign_row = (2 * signs[...] - 1).astype(jnp.float32)

    def close(c):
        full[low] = sum_x(0, c)
        full[1 - low] = sum_x(1, c)
        stacked = []
        for g in range(2):
            branch = full[g]
            stacked += [branch[:, b * HB : (b + 1) * HB] for b in range(per)]
        back = jnp.dot(
            split3(jnp.concatenate(stacked, axis=0)), had[...], preferred_element_type=jnp.float32
        ) * (1.0 / math.sqrt(HB))
        for g in range(2):
            at = slice(g * HALF + c * CW, g * HALF + (c + 1) * CW)
            pieces_of = []
            for j in range(SUB):
                for b in range(per):
                    row = (g * per + b) * PR + j * ROWS
                    pieces_of.append(back[row : row + ROWS])
            mixed[0, :, at] = (
                resid[0, :, at].astype(jnp.float32)
                + sign_row[:, at] * jnp.concatenate(pieces_of, axis=1)
            ).astype(jnp.bfloat16)

    def out_rows(ks, c):
        columns = pl.ds(c * CW, CW)
        spots = [(h, shift(pos_y(h), FAR_FIRST[k], 4)) for k in ks for h in range(2)]
        total = None
        for kind in range(2):
            left = jnp.concatenate([att[kind, h, j] for h, j in spots], axis=0)
            term = jnp.dot(left, wo[kind, :, columns], preferred_element_type=jnp.float32)
            total = term if total is None else total + term
        for n, (h, j) in enumerate(spots):
            parts[h, j, c] = total[n * PR : (n + 1) * PR].astype(jnp.bfloat16)

    for h in range(2):
        att_copy(h, 0).wait_recv()
    for c in range(NC):
        out_rows((0,), c)
        for h in range(2):
            send_raw(*ring1, h, c)
    for k in (1, 2, 3):
        for h in range(2):
            att_copy(h, k).wait_recv()
    for c0 in (0, 2):
        for c in (c0, c0 + 1):
            out_rows((1, 2, 3), c)
            for h in range(2):
                send_fin(*ring1, h, c, 1 if c % 2 == 0 else 0)
        for c in (c0, c0 + 1):
            for h in range(2):
                pass_on(*ring1, h, c)
    for c in range(NC):
        for h in range(2):
            done = finish(*ring1, h, c)
            for i in range(4):
                parts2[h, i, c] = jnp.concatenate(
                    [
                        done[i * ROWS : (i + 1) * ROWS, j * SW : (j + 1) * SW]
                        for j in range(SUB)
                    ],
                    axis=0,
                ).astype(jnp.bfloat16)
        scatter_x(c)
        if c > 0:
            close(c - 1)
    close(NC - 1)
    for copy in started:
        copy.wait_send()


def vmem(shape, dtype):
    return pltpu.VMEM(shape, dtype)


def shards(resid, norm_gain, signs, query_weight, kv_weight, out_weight, lengths):
    bf16, f32 = jnp.bfloat16, jnp.float32
    dma = pltpu.SemaphoreType.DMA
    in_vmem = pl.BlockSpec(memory_space=pltpu.VMEM)
    in_hbm = pl.BlockSpec(memory_space=pltpu.HBM)
    order = token_order()
    inverse = np.exp(np.arange(HD // 2) * (-2.0 * math.log(rope_base) / HD))
    angles = inverse[:, None] * order[None, :]
    table = np.zeros((HD // 2 + 8, 2 * TOK + HB))
    table[: HD // 2, :TOK] = np.cos(angles)
    table[: HD // 2, TOK : 2 * TOK] = np.sin(angles)
    table[HD // 2, : 2 * TOK] = np.concatenate([order, order])
    table[: HD // 2, 2 * TOK :] = inverse[:, None]
    ring = dma((2, 3, NC))
    return pl.pallas_call(
        sublayer_kernel,
        out_shape=jax.ShapeDtypeStruct(resid.shape, bf16),
        in_specs=[in_hbm] * 8,
        out_specs=in_vmem,
        scratch_shapes=[
            pltpu.SMEM((BLOCKS,), jnp.int32),
            vmem(resid.shape, bf16),
            vmem((1, D), f32),
            vmem((1, D), jnp.int32),
            vmem(table.shape, f32),
            vmem((3 * HB, HB), bf16),
            vmem((TOK, HB), f32),
            vmem((2, HALF, QC), bf16),
            vmem((2, KC, HALF), bf16),
            vmem((2, QC, HALF), bf16),
            vmem((2, NC, PR, SW), bf16),
            vmem((2, 4, 4, NC, PR, SW), bf16),
            vmem((4, 2, PR, HALF), bf16),
            vmem((2, 4, PR, QC), f32),
            vmem((2, 4, PR, 2 * KC), f32),
            vmem((2, 4, PR, QC), bf16),
            vmem((2, 4, PR, 2 * KC), bf16),
            vmem((2, 4, PR, QC), bf16),
            vmem((2, 4, PR, 2 * KC), bf16),
            vmem((HD, 2 * TOK), bf16),
            vmem((HD // 2, HB), f32),
            vmem((HD // 2, HB), f32),
            vmem((2, 2, 8, KC, TOK), bf16),
            vmem((1, 2 * TOK), f32),
            vmem((1, 2 * TOK), f32),
            vmem((HD, 2 * TOK), f32),
            vmem((2, 2, 4, PR, QC), bf16),
            vmem((2, 4, NC, PR, CW), bf16),
            vmem((2, NC, PR, CW), bf16),
            vmem((2, 2, NC, PR, CW), bf16),
            vmem((2, 4, NC, PR, SW), bf16),
            vmem((2, 4, NC, PR, SW), bf16),
            vmem((2, PR, SW), f32),
            dma((5,)),
            dma((3,)),
            dma((4, 2)),
            dma((4, 2)),
            dma((6,)),
            dma((6,)),
            dma,
            dma,
            dma((2, 3)),
            dma((2, 3)),
            dma((2, 3, 4)),
            dma((2, 3, 4)),
            dma((2, 2, 4)),
            dma((2, 2, 4)),
            dma((8,)),
            dma((8,)),
            dma((7,)),
            dma((7,)),
            dma((2, 8)),
            dma((2, 8)),
            dma((2, 4)),
            dma((2, 4)),
            ring,
            ring,
            dma((2, 4, NC)),
            dma((2, 4, NC)),
        ],
        compiler_params=pltpu.CompilerParams(
            collective_id=1, has_side_effects=True, vmem_limit_bytes=60 << 20
        ),
        name="sublayer",
    )(
        lengths, resid, norm_gain[None, :], signs[None, :], jnp.asarray(table, f32),
        query_weight, kv_weight.T, out_weight,
    )


def solution(mesh):
    return jax.shard_map(
        shards,
        mesh=mesh,
        in_specs=(
            P("section", "tensor", None),
            P(),
            P(),
            P(None, "tensor"),
            P(None, "tensor"),
            P("tensor", None),
            P(),
        ),
        out_specs=P("section", "tensor", None),
        check_vma=False,
    )
```

```python
import functools
import math

import jax
import jax.numpy as jnp
import numpy as np
from jax import lax
from jax.experimental import pallas as pl
from jax.experimental.pallas import tpu as pltpu
from jax.sharding import PartitionSpec as P

MESH = pl.DeviceIdType.MESH
D = 8192
HD = 128
HB = 128
ROWS = 12
TOK = 384
BLOCKS = 8
NC = 2
HALF = D // 2
CW = HALF // NC
SUB = 4
SW = CW // SUB
PR = SUB * ROWS
QC = 256
KC = 64
rope_base = 500000.0
norm_eps = 1e-05
NEG = -1e30


def token_order():
    order = []
    for half in range(2):
        for i in range(4):
            for j in range(4):
                y, x = (j, i) if half == 0 else (i, j)
                t = (y * 4 + x) * 2 + half
                order.extend(range(t * ROWS, (t + 1) * ROWS))
    return np.array(order)


def here():
    t = lax.axis_index("tensor")
    s = lax.axis_index("section")
    y = t // 8
    x = lax.rem(t // 2, 4)
    z = (s // 2) * 2 + lax.rem(t, 2)
    return y, x, z, lax.rem(s, 2)


def device(y, x, z, c):
    return ((y * 4 + x) * 2 + lax.rem(z, 2), (z // 2) * 2 + c)


def shift(value, by, size):
    return lax.rem(value + (by + size), size)


def split3(value):
    high = value.astype(jnp.bfloat16)
    rest = value - high.astype(jnp.float32)
    middle = rest.astype(jnp.bfloat16)
    low = (rest - middle.astype(jnp.float32)).astype(jnp.bfloat16)
    return jnp.concatenate([high, middle, low], axis=1)


def greet(partners):
    barrier = pltpu.get_barrier_semaphore()
    for partner in partners:
        pl.semaphore_signal(barrier, inc=1, device_id=partner, device_id_type=MESH)


def met(partners):
    pl.semaphore_wait(pltpu.get_barrier_semaphore(), len(partners))


def remote(src, dst, send, recv, target):
    return pltpu.make_async_remote_copy(
        src_ref=src,
        dst_ref=dst,
        send_sem=send,
        recv_sem=recv,
        device_id=target,
        device_id_type=MESH,
    )


def sublayer_kernel(
    lengths_hbm, resid_hbm, gain_hbm, signs_hbm, table_hbm, q_hbm, kv_hbm, out_hbm, mixed,
    lengths, resid, gain, signs, table, had, key_tok, wq, wkv, wo, rot, pieces, rows_ref, acc_q, acc_kv, cross_q, cross_kv, crossed_q, crossed_kv, queries, off_cos, off_sin,
    kvs, top_ref, total_ref, acc, att, parts, raw1, fin1, parts2, fin2, sums, last_z, own_sum, full,
    in_sem, w_sem, swq, rwq, swo, rwo, sa, ra, sg2, rg2, sg3, rg3, scr, rcr, sx, rx, skv, rkv, sc, rc,
    sat, rat, s1, r1, s2, r2,
):
    y, x, z, core = here()
    low = lax.rem(z, 2)
    high = z // 2
    section = lax.axis_index("section")
    toward = 1 - 2 * low

    def at_x(by):
        return device(y, shift(x, by, 4), z, core)

    def at_y(by):
        return device(shift(y, by, 4), x, z, core)

    def at_z(by):
        return device(y, x, shift(z, by, 8), core)

    mate = at_z(toward)
    other_core = device(y, x, z, 1 - core)
    own_x = lax.rem(x, 2)

    def x_mate_at(by):
        return device(y, x + 1 - 2 * own_x, shift(z, by, 8), core)

    x_mate = x_mate_at(0)

    def ring_x(h, by):
        return device(shift(y, by * h, 4), shift(x, by * (1 - h), 4), z, core)

    def ring_y(h, by):
        return device(shift(y, by * (1 - h), 4), shift(x, by * h, 4), z, core)

    def pos_x(h):
        return x * (1 - h) + y * h

    def pos_y(h):
        return y * (1 - h) + x * h

    started = []

    def go(copy):
        copy.start()
        started.append(copy)

    def settle():
        for copy in started:
            copy.wait_send()
        started.clear()

    partners = [at_z(by) for by in (1, -1, 2, -2)] + [other_core]
    partners += [at_x(by) for by in (1, -1, 2)] + [at_y(by) for by in (1, -1, 2)]
    partners += [x_mate_at(by) for by in (1, -1, 2, -2)]
    greet(partners)
    inputs = [
        pltpu.make_async_copy(from_, to, in_sem.at[k])
        for k, (from_, to) in enumerate(
            [
                (resid_hbm, resid), (gain_hbm, gain), (signs_hbm, signs), (lengths_hbm, lengths),
                (table_hbm, table),
            ]
        )
    ]
    for copy in inputs:
        copy.start()

    mine = pl.multiple_of(low * HALF, HALF)
    loads = [
        pltpu.make_async_copy(q_hbm.at[pl.ds(mine, HALF)], wq.at[0], w_sem.at[0]),
        pltpu.make_async_copy(kv_hbm.at[:, pl.ds(mine, HALF)], wkv.at[0], w_sem.at[1]),
        pltpu.make_async_copy(out_hbm.at[:, pl.ds(mine, HALF)], wo.at[0], w_sem.at[2]),
    ]
    QTR = HALF // 4

    def quarter(way, c):
        return (way * 2 + c) * QTR

    def ship_proj(way):
        target = at_z(toward * (1 - 2 * way))
        off = quarter(way, core)
        from_ = pl.multiple_of((1 - low) * HALF + off, QTR)
        to = pl.multiple_of(off, QTR)
        go(remote(q_hbm.at[pl.ds(from_, QTR)], wq.at[1, pl.ds(to, QTR)], swq.at[way, 0], rwq.at[way, 0], target))
        go(remote(kv_hbm.at[:, pl.ds(from_, QTR)], wkv.at[1, :, pl.ds(to, QTR)], swq.at[way, 1], rwq.at[way, 1], target))

    def share_proj(way):
        to = pl.multiple_of(quarter(way, core), QTR)
        q_ref, kv_ref = wq.at[1, pl.ds(to, QTR)], wkv.at[1, :, pl.ds(to, QTR)]
        remote(q_ref, q_ref, swq.at[way, 0], rwq.at[way, 0], mate).wait_recv()
        remote(kv_ref, kv_ref, swq.at[way, 1], rwq.at[way, 1], mate).wait_recv()
        go(remote(q_ref, q_ref, swq.at[2 + way, 0], rwq.at[2 + way, 0], other_core))
        go(remote(kv_ref, kv_ref, swq.at[2 + way, 1], rwq.at[2 + way, 1], other_core))

    def shared_proj(way):
        to = pl.multiple_of(quarter(way, 1 - core), QTR)
        q_ref, kv_ref = wq.at[1, pl.ds(to, QTR)], wkv.at[1, :, pl.ds(to, QTR)]
        remote(q_ref, q_ref, swq.at[2 + way, 0], rwq.at[2 + way, 0], other_core).wait_recv()
        remote(kv_ref, kv_ref, swq.at[2 + way, 1], rwq.at[2 + way, 1], other_core).wait_recv()

    def out_part(part, c):
        start = quarter(1, c) if part == 0 else quarter(0, c) + (part - 1) * (QTR // 2)
        return start, QTR if part == 0 else QTR // 2

    def ship_out(part):
        target = at_z(toward if part == 1 else -toward)
        start, width = out_part(part, core)
        from_ = pl.multiple_of((1 - low) * HALF + start, width)
        to = pl.multiple_of(start, width)
        go(remote(out_hbm.at[:, pl.ds(from_, width)], wo.at[1, :, pl.ds(to, width)], swo.at[part], rwo.at[part], target))

    def share_out(part):
        start, width = out_part(part, core)
        ref = wo.at[1, :, pl.ds(pl.multiple_of(start, width), width)]
        remote(ref, ref, swo.at[part], rwo.at[part], mate).wait_recv()
        go(remote(ref, ref, swo.at[3 + part], rwo.at[3 + part], other_core))

    def shared_out(part):
        start, width = out_part(part, 1 - core)
        ref = wo.at[1, :, pl.ds(pl.multiple_of(start, width), width)]
        remote(ref, ref, swo.at[3 + part], rwo.at[3 + part], other_core).wait_recv()

    for load in loads:
        load.start()
    row = lax.broadcasted_iota(jnp.int32, (HB, HB), 0)
    column = lax.broadcasted_iota(jnp.int32, (HB, HB), 1)
    odd = row & column
    for bits in (4, 2, 1):
        odd = odd ^ (odd >> bits)
    signed = (1 - 2 * (odd & 1)).astype(jnp.float32).astype(jnp.bfloat16)
    for k in range(3):
        had[k * HB : (k + 1) * HB] = signed
    for copy in inputs[:3]:
        copy.wait()

    stream = resid[0].astype(jnp.float32)
    sign_row = (2 * signs[...] - 1).astype(jnp.float32)
    normed = (
        stream
        * lax.rsqrt(jnp.mean(stream * stream, axis=-1, keepdims=True) + norm_eps)
        * gain[...]
        * sign_row
    )
    per = SW // HB
    stacked = []
    for g in range(2 * NC):
        for b in range(per):
            stacked.append(
                jnp.concatenate(
                    [
                        normed[:, g * CW + j * SW + b * HB : g * CW + j * SW + (b + 1) * HB]
                        for j in range(SUB)
                    ],
                    axis=0,
                )
            )
    rotated = jnp.dot(
        split3(jnp.concatenate(stacked, axis=0)), had[...], preferred_element_type=jnp.float32
    ) * (1.0 / math.sqrt(HB))
    for g in range(2 * NC):
        blocks_of = [rotated[(g * per + b) * PR : (g * per + b + 1) * PR] for b in range(per)]
        rot[g // NC, g % NC] = jnp.concatenate(blocks_of, axis=1).astype(jnp.bfloat16)

    met(partners)

    STEP = (0, -1, 1, 2)

    def piece(h, dj, di):
        return pieces.at[h, shift(pos_y(h), dj, 4), shift(pos_x(h), di, 4)]

    def swap_copy(h):
        return remote(rot.at[1 - low], piece(h, 0, 0), sa, ra, mate)

    def spread_x(h):
        ref = piece(h, 0, 0)
        for k in (1, 2, 3):
            go(remote(ref, ref, sg2.at[h, k - 1], rg2.at[h, k - 1], ring_x(h, -STEP[k])))

    def spread_y(h, k):
        ref = piece(h, 0, STEP[k])
        for kind, by in ((0, 1), (1, -1)):
            go(remote(ref, ref, sg3.at[h, kind, k], rg3.at[h, kind, k], ring_y(h, by)))

    def from_x(h, k):
        ref = piece(h, 0, STEP[k])
        remote(ref, ref, sg2.at[h, k - 1], rg2.at[h, k - 1], mate).wait_recv()

    def from_y(h, k):
        for kind, by in ((0, -1), (1, 1)):
            ref = piece(h, by, STEP[k])
            remote(ref, ref, sg3.at[h, kind, k], rg3.at[h, kind, k], mate).wait_recv()
        by = -1 if k in (0, 3) else 1
        ref = piece(h, by, STEP[k])
        go(remote(ref, ref, sg3.at[h, 2, k], rg3.at[h, 2, k], ring_y(h, -by)))

    def from_far(h, k):
        ref = piece(h, 2, STEP[k])
        remote(ref, ref, sg3.at[h, 2, k], rg3.at[h, 2, k], mate).wait_recv()

    pieces[low, pos_y(low), pos_x(low)] = rot[low]
    go(swap_copy(low))
    ship_proj(1)
    spread_x(low)
    spread_y(low, 0)
    ship_proj(0)
    swap_copy(1 - low).wait_recv()
    spread_x(1 - low)
    spread_y(1 - low, 0)
    high_half = 1 - low
    for k in (1, 2, 3):
        from_x(low, k)
        spread_y(low, k)
    from_y(low, 0)
    for k in (1, 2, 3):
        from_x(high_half, k)
        spread_y(high_half, k)
    from_y(low, 1)
    from_y(high_half, 0)
    ship_out(0)
    ship_out(2)
    from_y(low, 2)
    from_y(high_half, 1)
    for load in loads:
        load.wait()

    def join(k):
        for h in range(2):
            i = shift(pos_x(h), STEP[k], 4)
            for c in range(NC):
                parts_of = [pieces[h, j, i, c].astype(jnp.float32) for j in range(4)]
                rows_ref[k, h, :, c * CW : (c + 1) * CW] = jnp.concatenate(
                    [
                        jnp.concatenate(
                            [part[u * ROWS : (u + 1) * ROWS] for part in parts_of], axis=0
                        )
                        for u in range(SUB)
                    ],
                    axis=1,
                ).astype(jnp.bfloat16)

    def group(k):
        return rows_ref[k].reshape(2 * PR, HALF)

    def add_own():
        part = jnp.dot(
            rows_ref[...].reshape(8 * PR, HALF), wq[0], preferred_element_type=jnp.float32
        )
        for k in range(4):
            for h in range(2):
                start = (k * 2 + h) * PR
                acc_q[h, shift(pos_x(h), STEP[k], 4)] = part[start : start + PR]

    def add_mates(first):
        rows = rows_ref[first : first + 2].reshape(4 * PR, HALF)
        part = jnp.dot(rows, wq[1], preferred_element_type=jnp.float32)
        for k in (first, first + 1):
            for h in range(2):
                start = ((k - first) * 2 + h) * PR
                cross_q[h, shift(pos_x(h), STEP[k], 4)] = part[start : start + PR].astype(
                    jnp.bfloat16
                )
                go(cross_copy(1, h, k))

    def add_kv(k):
        part = lax.dot_general(
            group(k),
            wkv[...].reshape(2 * KC, HALF),
            (((1,), (1,)), ((), ())),
            preferred_element_type=jnp.float32,
        )
        for h in range(2):
            i = shift(pos_x(h), STEP[k], 4)
            acc_kv[h, i] = part[h * PR : (h + 1) * PR]
            cross_kv[h, i] = part[h * PR : (h + 1) * PR].astype(jnp.bfloat16)

    def cross_copy(kind, h, k):
        i = shift(pos_x(h), STEP[k], 4)
        src, dst = ((cross_kv, crossed_kv), (cross_q, crossed_q))[kind]
        return remote(src.at[h, i], dst.at[h, i], scr.at[kind, h, k], rcr.at[kind, h, k], mate)

    def cross_group(k):
        add_kv(k)
        for h in range(2):
            go(cross_copy(0, h, k))

    for copy in inputs[3:]:
        copy.wait()
    tok_cos = table.at[: HD // 2, :TOK]
    tok_sin = table.at[: HD // 2, TOK : 2 * TOK]
    query_tok = table.at[HD // 2 : HD // 2 + 1, : 2 * TOK]
    inverse = table.at[: HD // 2, 2 * TOK :]
    key_tok[...] = jnp.transpose(
        jnp.broadcast_to(table[HD // 2 : HD // 2 + 1, :TOK], (HB, TOK))
    )
    lane = lax.broadcasted_iota(jnp.int32, (1, HB), 1)
    starts = jnp.zeros((1, HB), jnp.int32)
    for b in range(BLOCKS - 1):
        starts = starts + jnp.where(lane > b, lengths[b], 0)
    angles = inverse[...] * starts.astype(jnp.float32)
    off_cos[...] = jnp.cos(angles)
    off_sin[...] = jnp.sin(angles)

    def rotary_table(index):
        here_only = lane == index
        oc = jnp.sum(jnp.where(here_only, off_cos[...], 0.0), axis=1, keepdims=True)
        os = jnp.sum(jnp.where(here_only, off_sin[...], 0.0), axis=1, keepdims=True)
        return oc * tok_cos[...] - os * tok_sin[...], os * tok_cos[...] + oc * tok_sin[...]

    def own_group(k):
        for h in range(2):
            from_far(h, k)
        join(k)

    own_group(0)
    from_y(low, 3)
    from_y(high_half, 2)
    share_proj(1)
    share_proj(0)
    ship_out(1)
    own_group(1)
    for way in range(2):
        shared_proj(way)
    cross_group(0)
    from_y(high_half, 3)
    cross_group(1)
    add_mates(0)
    own_group(2)
    cross_group(2)
    for h in range(2):
        from_far(h, 3)
    join(3)
    cross_group(3)
    add_mates(2)
    half = HD // 2

    def side(e):
        return own_x if e == 0 else 1 - own_x

    def kv_piece(e, by):
        return kvs.at[core, side(e), shift(z, by, 8)]

    def along(by, hops, kind):
        ref = kv_piece(0, by)
        return remote(ref, ref, skv.at[kind], rkv.at[kind], at_z(hops))

    def across(by, hops, kind):
        ref = kv_piece(0, by)
        return remote(ref, ref, sx.at[kind], rx.at[kind], x_mate_at(hops))

    def to_mates(by, x_too=True):
        ref = kv_piece(0, by)
        k = by % 8
        if x_too:
            go(remote(ref, ref, sx.at[k], rx.at[k], x_mate))
        go(remote(ref, ref, sc.at[0, k], rc.at[0, k], other_core))

    def from_x_mate(by):
        ref = kv_piece(1, by)
        k = by % 8
        remote(ref, ref, sx.at[k], rx.at[k], x_mate).wait_recv()
        go(remote(ref, ref, sc.at[1, k], rc.at[1, k], other_core))

    for k in range(4):
        for h in range(2):
            cross_copy(0, h, k).wait_recv()
    kv_sum = acc_kv[...].reshape(TOK, 2 * KC) + pltpu.roll(
        crossed_kv[...].astype(jnp.float32).reshape(TOK, 2 * KC), KC, 1
    )
    kvs[core, own_x, z] = jnp.transpose(kv_sum)[:KC].astype(jnp.bfloat16)
    go(along(0, 2, 2))
    go(along(0, -2, 3))
    go(along(0, 1, 0))
    go(along(0, -1, 1))
    to_mates(0)
    add_own()

    for k in range(4):
        for h in range(2):
            cross_copy(1, h, k).wait_recv()
    turned = jnp.transpose(
        (acc_q[...] + crossed_q[...].astype(jnp.float32)).reshape(TOK, QC)
    )
    cosine, sine = rotary_table(section)
    for head in range(2):
        first = turned[head * HD : head * HD + half]
        second = turned[head * HD + half : (head + 1) * HD]
        queries[:half, head * TOK : (head + 1) * TOK] = (
            first * cosine - second * sine
        ).astype(jnp.bfloat16)
        queries[half:, head * TOK : (head + 1) * TOK] = (
            second * cosine + first * sine
        ).astype(jnp.bfloat16)

    def from_core(back):
        for u in range(2):
            k = shift(u - low, 8 - 2 * back, 8)
            for e in range(2):
                ref = kvs.at[1 - core, side(e), lax.rem(z + k, 8)]
                remote(ref, ref, sc.at[e, k], rc.at[e, k], other_core).wait_recv()

    scale = math.log2(math.e) / math.sqrt(HD)

    def absorb(c, row, diagonal):
        index = row * 2 + c
        pair = pl.ds(row * 2, 2)
        raw = kvs[c, 0, pair].astype(jnp.float32)
        value = kvs[c, 1, pair].reshape(HD, TOK)
        cosine, sine = rotary_table(index)
        key = jnp.concatenate(
            [raw[0] * cosine - raw[1] * sine, raw[1] * cosine + raw[0] * sine], axis=0
        )
        key = jnp.transpose(key).astype(jnp.bfloat16)
        scores = jnp.dot(key, queries[...], preferred_element_type=jnp.float32)
        token = key_tok[:, :1]
        valid = token < lengths[index].astype(jnp.float32)
        if diagonal:
            seen = valid & (token <= query_tok[...])
            scores = jnp.where(seen, scores, NEG)
            top = jnp.max(scores, axis=0, keepdims=True)
            weights = jnp.exp2((scores - top) * scale)
            total_ref[...] = jnp.sum(weights, axis=0, keepdims=True)
            acc[...] = jnp.dot(
                value, weights.astype(jnp.bfloat16), preferred_element_type=jnp.float32
            )
        else:
            scores = scores + jnp.where(valid, 0.0, NEG)
            old = top_ref[...]
            top = jnp.maximum(old, jnp.max(scores, axis=0, keepdims=True))
            weights = jnp.exp2((scores - top) * scale)
            fade = jnp.exp2((old - top) * scale)
            total_ref[...] = total_ref[...] * fade + jnp.sum(weights, axis=0, keepdims=True)
            acc[...] = acc[...] * fade + jnp.dot(
                value, weights.astype(jnp.bfloat16), preferred_element_type=jnp.float32
            )
        top_ref[...] = top

    def earlier(back):
        @pl.when(high >= back)
        def _():
            for c in range(2):
                absorb(c, high - back, False)

    for by, kind in ((-2, 2), (2, 3)):
        along(by, 0, kind).wait_recv()
        on = 1 if by < 0 else -1
        go(along(by, on, 4 if by < 0 else 5))
        go(across(by, on, (by - on) % 8))
        to_mates(by)
    turn = 2 - 4 * core
    go(along(-turn, turn, 6))
    go(across(-turn, turn, 4))
    for by, kind in ((-1, 0), (1, 1)):
        along(by, 0, kind).wait_recv()
        to_mates(by)
    for by in (0, -2, 2, -1, 1):
        from_x_mate(by)
    from_core(0)
    absorb(core, high, True)

    @pl.when(core == 1)
    def _():
        absorb(0, high, False)

    near = 1 + 2 * low
    from_core(near)
    earlier(near)
    for by, kind in ((-3, 4), (3, 5), (4, 6)):
        along(by, 0, kind).wait_recv()
        to_mates(by, False)
    for by in (-3, 3, 4):
        from_x_mate(by)
    for part in range(3):
        share_out(part)
    for back in (4 - near, 2):
        from_core(back)
        earlier(back)
    attended = acc[...] / total_ref[...]
    for head in range(2):
        rows = jnp.transpose(attended[:, head * TOK : (head + 1) * TOK])
        for h in range(2):
            for j in range(4):
                att[0, h, j, :, head * HD : (head + 1) * HD] = jnp.concatenate(
                    [
                        rows[h * 4 * PR + i * PR + j * ROWS : h * 4 * PR + i * PR + (j + 1) * ROWS]
                        for i in range(4)
                    ],
                    axis=0,
                ).astype(jnp.bfloat16)
    def att_copy(h, k):
        j = shift(pos_y(h), FAR_FIRST[k], 4)
        return remote(att.at[0, h, j], att.at[1, h, j], sat.at[h, k], rat.at[h, k], mate)

    FAR_FIRST = (2, 1, -1, 0)
    for k in range(4):
        for h in range(2):
            go(att_copy(h, k))
    for part in range(3):
        shared_out(part)

    def send_raw(buf, raw, fin, pos, ssem, rsem, peer, h, c):
        by = 1 if c % 2 == 0 else -1
        go(
            remote(
                buf.at[h, shift(pos(h), 2, 4), c], raw.at[h, c], ssem.at[h, 2, c],
                rsem.at[h, 2, c], peer(h, by),
            )
        )

    def send_fin(buf, raw, fin, pos, ssem, rsem, peer, h, c, kind):
        by = 1 if kind == 0 else -1
        go(
            remote(
                buf.at[h, shift(pos(h), by, 4), c], fin.at[h, kind, c], ssem.at[h, kind, c],
                rsem.at[h, kind, c], peer(h, by),
            )
        )

    def pass_on(buf, raw, fin, pos, ssem, rsem, peer, h, c):
        kind, by = (0, 1) if c % 2 == 0 else (1, -1)
        ref = raw.at[h, c]
        remote(ref, ref, ssem.at[h, 2, c], rsem.at[h, 2, c], peer(h, 1)).wait_recv()
        slot = shift(pos(h), by, 4)
        buf[h, slot, c] = (
            buf[h, slot, c].astype(jnp.float32) + raw[h, c].astype(jnp.float32)
        ).astype(jnp.bfloat16)
        send_fin(buf, raw, fin, pos, ssem, rsem, peer, h, c, kind)

    def finish(buf, raw, fin, pos, ssem, rsem, peer, h, c):
        for kind in range(2):
            ref = fin.at[h, kind, c]
            remote(ref, ref, ssem.at[h, kind, c], rsem.at[h, kind, c], peer(h, 1)).wait_recv()
        return (
            buf[h, pos(h), c].astype(jnp.float32)
            + fin[h, 0, c].astype(jnp.float32)
            + fin[h, 1, c].astype(jnp.float32)
        )

    ring1 = (parts, raw1, fin1, pos_y, s1, r1, ring_y)

    def scatter_x(c):
        for h in range(2):
            for k in (1, 2, 3):
                go(
                    remote(
                        parts2.at[h, shift(pos_x(h), -STEP[k], 4), c], fin2.at[h, k, c],
                        s2.at[h, k, c], r2.at[h, k, c], ring_x(h, -STEP[k]),
                    )
                )

    def sum_x(h, c):
        done = parts2[h, pos_x(h), c].astype(jnp.float32)
        for k in (1, 2, 3):
            ref = fin2.at[h, k, c]
            remote(ref, ref, s2.at[h, k, c], r2.at[h, k, c], mate).wait_recv()
            done = done + fin2[h, k, c].astype(jnp.float32)
        return done

    def z_copy(c):
        return remote(sums.at[c], last_z.at[c], s2.at[0, 0, c], r2.at[0, 0, c], mate)

    def swap(c):
        sums[c] = sum_x(1 - low, c).astype(jnp.bfloat16)
        go(z_copy(c))
        own_sum[c] = sum_x(low, c)

    sign_row = (2 * signs[...] - 1).astype(jnp.float32)

    def close(c):
        z_copy(c).wait_recv()
        full[low] = own_sum[c]
        full[1 - low] = last_z[c].astype(jnp.float32)
        stacked = []
        for g in range(2):
            branch = full[g]
            stacked += [branch[:, b * HB : (b + 1) * HB] for b in range(per)]
        back = jnp.dot(
            split3(jnp.concatenate(stacked, axis=0)), had[...], preferred_element_type=jnp.float32
        ) * (1.0 / math.sqrt(HB))
        for g in range(2):
            at = slice(g * HALF + c * CW, g * HALF + (c + 1) * CW)
            pieces_of = []
            for j in range(SUB):
                for b in range(per):
                    row = (g * per + b) * PR + j * ROWS
                    pieces_of.append(back[row : row + ROWS])
            mixed[0, :, at] = (
                resid[0, :, at].astype(jnp.float32)
                + sign_row[:, at] * jnp.concatenate(pieces_of, axis=1)
            ).astype(jnp.bfloat16)

    def out_rows(ks, c):
        columns = pl.ds(c * CW, CW)
        spots = [(h, shift(pos_y(h), FAR_FIRST[k], 4)) for k in ks for h in range(2)]
        total = None
        for kind in range(2):
            left = jnp.concatenate([att[kind, h, j] for h, j in spots], axis=0)
            term = jnp.dot(left, wo[kind, :, columns], preferred_element_type=jnp.float32)
            total = term if total is None else total + term
        for n, (h, j) in enumerate(spots):
            parts[h, j, c] = total[n * PR : (n + 1) * PR].astype(jnp.bfloat16)

    early = list(started)
    started.clear()
    for h in range(2):
        att_copy(h, 0).wait_recv()
    for c in range(NC):
        out_rows((0,), c)
        for h in range(2):
            send_raw(*ring1, h, c)
    for copy in early:
        copy.wait_send()
    for k in (1, 2, 3):
        for h in range(2):
            att_copy(h, k).wait_recv()
    for c0 in range(0, NC, 2):
        for c in (c0, c0 + 1):
            out_rows((1, 2, 3), c)
            for h in range(2):
                send_fin(*ring1, h, c, 1 if c % 2 == 0 else 0)
        for c in (c0, c0 + 1):
            for h in range(2):
                pass_on(*ring1, h, c)
    for c in range(NC):
        for h in range(2):
            done = finish(*ring1, h, c)
            for i in range(4):
                parts2[h, i, c] = jnp.concatenate(
                    [
                        done[i * ROWS : (i + 1) * ROWS, j * SW : (j + 1) * SW]
                        for j in range(SUB)
                    ],
                    axis=0,
                ).astype(jnp.bfloat16)
        if c == NC - 1:
            early = list(started)
            started.clear()
        scatter_x(c)
        if c > 0:
            swap(c - 1)
        if c > 1:
            close(c - 2)
    for copy in early:
        copy.wait_send()
    swap(NC - 1)
    close(NC - 2)
    close(NC - 1)
    settle()


def vmem(shape, dtype):
    return pltpu.VMEM(shape, dtype)


def shards(resid, norm_gain, signs, query_weight, kv_weight, out_weight, lengths):
    bf16, f32 = jnp.bfloat16, jnp.float32
    dma = pltpu.SemaphoreType.DMA
    in_vmem = pl.BlockSpec(memory_space=pltpu.VMEM)
    in_hbm = pl.BlockSpec(memory_space=pltpu.HBM)
    order = token_order()
    inverse = np.exp(np.arange(HD // 2) * (-2.0 * math.log(rope_base) / HD))
    angles = inverse[:, None] * order[None, :]
    table = np.zeros((HD // 2 + 8, 2 * TOK + HB))
    table[: HD // 2, :TOK] = np.cos(angles)
    table[: HD // 2, TOK : 2 * TOK] = np.sin(angles)
    table[HD // 2, : 2 * TOK] = np.concatenate([order, order])
    table[: HD // 2, 2 * TOK :] = inverse[:, None]
    ring = dma((2, 3, NC))
    return pl.pallas_call(
        sublayer_kernel,
        out_shape=jax.ShapeDtypeStruct(resid.shape, bf16),
        in_specs=[in_hbm] * 8,
        out_specs=in_vmem,
        scratch_shapes=[
            pltpu.SMEM((BLOCKS,), jnp.int32),
            vmem(resid.shape, bf16),
            vmem((1, D), f32),
            vmem((1, D), jnp.int32),
            vmem(table.shape, f32),
            vmem((3 * HB, HB), bf16),
            vmem((TOK, HB), f32),
            vmem((2, HALF, QC), bf16),
            vmem((2, KC, HALF), bf16),
            vmem((2, QC, HALF), bf16),
            vmem((2, NC, PR, SW), bf16),
            vmem((2, 4, 4, NC, PR, SW), bf16),
            vmem((4, 2, PR, HALF), bf16),
            vmem((2, 4, PR, QC), f32),
            vmem((2, 4, PR, 2 * KC), f32),
            vmem((2, 4, PR, QC), bf16),
            vmem((2, 4, PR, 2 * KC), bf16),
            vmem((2, 4, PR, QC), bf16),
            vmem((2, 4, PR, 2 * KC), bf16),
            vmem((HD, 2 * TOK), bf16),
            vmem((HD // 2, HB), f32),
            vmem((HD // 2, HB), f32),
            vmem((2, 2, 8, KC, TOK), bf16),
            vmem((1, 2 * TOK), f32),
            vmem((1, 2 * TOK), f32),
            vmem((HD, 2 * TOK), f32),
            vmem((2, 2, 4, PR, QC), bf16),
            vmem((2, 4, NC, PR, CW), bf16),
            vmem((2, NC, PR, CW), bf16),
            vmem((2, 2, NC, PR, CW), bf16),
            vmem((2, 4, NC, PR, SW), bf16),
            vmem((2, 4, NC, PR, SW), bf16),
            vmem((NC, PR, SW), bf16),
            vmem((NC, PR, SW), bf16),
            vmem((NC, PR, SW), f32),
            vmem((2, PR, SW), f32),
            dma((5,)),
            dma((3,)),
            dma((4, 2)),
            dma((4, 2)),
            dma((6,)),
            dma((6,)),
            dma,
            dma,
            dma((2, 3)),
            dma((2, 3)),
            dma((2, 3, 4)),
            dma((2, 3, 4)),
            dma((2, 2, 4)),
            dma((2, 2, 4)),
            dma((8,)),
            dma((8,)),
            dma((7,)),
            dma((7,)),
            dma((2, 8)),
            dma((2, 8)),
            dma((2, 4)),
            dma((2, 4)),
            ring,
            ring,
            dma((2, 4, NC)),
            dma((2, 4, NC)),
        ],
        compiler_params=pltpu.CompilerParams(
            collective_id=1, has_side_effects=True, vmem_limit_bytes=60 << 20
        ),
        name="sublayer",
    )(
        lengths, resid, norm_gain[None, :], signs[None, :], jnp.asarray(table, f32),
        query_weight, kv_weight.T, out_weight,
    )


def solution(mesh):
    return jax.shard_map(
        shards,
        mesh=mesh,
        in_specs=(
            P("section", "tensor", None),
            P(),
            P(),
            P(None, "tensor"),
            P(None, "tensor"),
            P("tensor", None),
            P(),
        ),
        out_specs=P("section", "tensor", None),
        check_vma=False,
    )
```
